512 devices in a mesh: replica: 16 (over x, z_hi, core), fsdp: 32 (over y, z_lo).
Axes of the slice: x: 4, y: 4, z: 16 (z_hi: 2, z_lo: 8; z = z_hi * 8 + z_lo), core: 2. Of those that a mesh axis runs over, the one named last changes fastest.
Arguments:
- tokens: bfloat16 [16, 4096, 8192], P('replica', 'fsdp'), may hold values from -6 to 6
- norm_gain: bfloat16 [8192], replicated, may hold values from 0.099609375 to 1.8984375
- cotangent: bfloat16 [16, 4096, 1024], P('replica', 'fsdp'), may hold values from -6 to 6
- layer_weight: bfloat16 [16, 8192, 1024], P('replica', 'fsdp'), may hold values from -0.09375 to 0.09375
- shared_copy: bfloat16 [8192, 1024], P('fsdp'), may hold values from -0.0625 to 0.0625
- master: float32 [8192, 1024], P('fsdp', 'replica'), may hold values from -0.0625 to 0.0625
- momentum: float32 [8192, 1024], P('fsdp', 'replica'), may hold values from -0.078125 to 0.078125
Outputs:
- layer_next: bfloat16 [16, 8192, 1024], P('replica', 'fsdp')
- master_next: float32 [8192, 1024], P('fsdp', 'replica')
- momentum_next: float32 [8192, 1024], P('fsdp', 'replica')
The draws below stay inside these ranges and needn't reach their ends.
All inputs are finite; a program needn't handle non-finite values.
Results may differ from the reference program's by a relative error of at most 0.013.
Values may be sent and summed in bfloat16 or wider, within the bound.
A program may use at most 64 MiB of HBM per device.

```python
import math
import jax
import jax.numpy as jnp
from jax import lax

D = 8192
KV = 512
BLOCK = 64
TOKENS_REP = 4096
REPLICAS = 16


def spiked(drawn, stream_key, source, target, parts, factor):
    def block_of(dim):
        return (jnp.arange(drawn.shape[dim]) // (drawn.shape[dim] // parts)).reshape((-1,) + (1,) * (drawn.ndim - 1 - dim))

    first = jax.random.permutation(stream_key, parts)[block_of(target)]
    far = (block_of(target) + parts // 2) % parts
    return jnp.where((block_of(source) == first) | (block_of(source) == far), factor * drawn, drawn)


def block_levels(own_key, extent, cuts, least, high):
    level, own = 1.0, jax.random.fold_in(own_key, 6)
    for position, shards_of in cuts:
        draws = jnp.exp(jax.random.uniform(jax.random.fold_in(own, position), (shards_of,), jnp.float32, least / len(cuts), high / len(cuts)))
        level = level * jnp.repeat(draws, extent[position] // shards_of).reshape([-1 if axis == position else 1 for axis in range(len(extent))])
    return level


def centred(stream_key, extent, spread, limit, cuts=(), kind=jnp.bfloat16):
    level = block_levels(stream_key, extent, cuts, -0.22, 0.18) if cuts else 1.0
    entries = jax.random.normal(stream_key, extent, jnp.float32) * spread * level
    return jnp.minimum(jnp.maximum(entries, -limit), limit).astype(kind)


def noise_with(key, dims, spread, reach, shards, heavy, dtype=jnp.bfloat16):
    result = spread * jax.random.normal(key, dims, jnp.float32)
    if shards:
        result = result * block_levels(key, dims, shards, -0.22, 0.18)
    return jnp.clip(spiked(result, jax.random.fold_in(key, 3), *heavy), -reach, reach).astype(dtype)


def setup_inputs(seed: int = 0) -> dict:
    splits = jax.random.split(jax.random.key(seed), 8)
    tokens = centred(splits[0], (REPLICAS, TOKENS_REP, D), 1.0, 6.0, ((0, 16), (1, 32)))
    norm_gain = jnp.clip(1.0 + 0.18 * jax.random.normal(splits[1], (D,), jnp.float32), 0.099609375, 1.8984375).astype(jnp.bfloat16)
    cotangent = centred(splits[2], (REPLICAS, TOKENS_REP, 2 * KV), 1.0, 6.0, ((0, 16), (1, 32)))
    layer_weight = noise_with(splits[3], (REPLICAS, D, 2 * KV), D ** -0.5, 0.09375, ((0, 16), (1, 32)), (0, 2, 16, 2.0))
    shared_copy = centred(splits[4], (D, 2 * KV), D ** -0.5, 0.0625, ((0, 32),))
    master = centred(splits[5], (D, 2 * KV), D ** -0.5, 0.0625, ((0, 32), (1, 16)), jnp.float32)
    momentum = centred(splits[6], (D, 2 * KV), 0.005, 0.078125, ((0, 32), (1, 16)), jnp.float32)
    return dict(tokens=tokens, norm_gain=norm_gain, cotangent=cotangent, layer_weight=layer_weight, shared_copy=shared_copy, master=master, momentum=momentum)


norm_eps = 1e-05
inner_gain = 0.4
outer_rate = 0.7
outer_beta = 0.9
mix_weight = 0.5
code_range = 448.0

def reference(tokens, norm_gain, cotangent, layer_weight, shared_copy, master, momentum):
    shared_float = shared_copy.astype(jnp.float32)
    inner_rate = inner_gain / math.sqrt(TOKENS_REP)

    def replica_work(inputs):
        tok_block, cot_block, weight_block = inputs
        tok_float = tok_block.astype(jnp.float32)
        inverse = lax.rsqrt(lax.optimization_barrier(jnp.mean(tok_float * tok_float, axis=-1, keepdims=True)) + norm_eps)
        normed = (tok_float * inverse * norm_gain.astype(jnp.float32)).astype(jnp.bfloat16)
        grad = jnp.einsum('td,tk->dk', normed.astype(jnp.float32), cot_block.astype(jnp.float32))
        weight_float = weight_block.astype(jnp.float32)
        stepped = weight_float - inner_rate * grad
        delta = (shared_float - weight_float).reshape(D, 2 * KV // BLOCK, BLOCK)
        largest = lax.optimization_barrier(jnp.max(jnp.abs(delta), axis=-1, keepdims=True))
        scale = ((largest + 1e-06) / code_range).astype(jnp.bfloat16)
        coded = (delta / scale.astype(jnp.float32)).astype(jnp.bfloat16)
        decoded = coded.astype(jnp.float32) * scale.astype(jnp.float32)
        return (stepped, decoded.reshape(D, 2 * KV))
    stepped, decoded = lax.map(replica_work, (tokens, cotangent, layer_weight))
    average = lax.optimization_barrier(jnp.sum(decoded, axis=0)) / REPLICAS
    momentum_next = outer_beta * momentum + average
    master_next = master - outer_rate * (average + outer_beta * momentum_next)
    shared_next = master_next.astype(jnp.bfloat16).astype(jnp.float32)
    layer_next = (mix_weight * stepped + (1.0 - mix_weight) * shared_next[None]).astype(jnp.bfloat16)
    return (layer_next, master_next, momentum_next)
```

```python
import functools
import math

import jax
import jax.numpy as jnp
from jax import lax
from jax.experimental import pallas as pl
from jax.experimental.pallas import tpu as pltpu
from jax.sharding import PartitionSpec as P

BLOCK = 64
norm_eps = 1e-05
inner_gain = 0.4
outer_rate = 0.7
outer_beta = 0.9
mix_weight = 0.5
code_range = 448.0

NX, NY, NZ = 4, 4, 8
REPLICAS = 16
MESH = pl.DeviceIdType.MESH
F32, BF16 = jnp.float32, jnp.bfloat16
COLS = 256
SUBS = 4
UNITS = (NZ - 1) * SUBS
DEPTH = 3


def kernel(
    tok_hbm, gain_ref, cot_hbm, w_hbm, shared_hbm, master_hbm, mom_hbm,
    layer_out, master_out, mom_out,
    tok, cot, w, shared, master, mom,
    tokg, cotg, buf_f, buf_b, dec, x_in, half, core_out, core_in, z_out, z_in,
    full, pair_out, pair_in, sh, sh_in,
    load_sem, st, rt, sc, rc, sf, rf, sb, rb, sx, rx, sg, rg, ss, rs,
):
    rep, fs = lax.axis_index("replica"), lax.axis_index("fsdp")
    x, zh, c = rep // 4, lax.rem(rep // 2, 2), lax.rem(rep, 2)
    y, z = fs // NZ, lax.rem(fs, NZ)

    def device(x=x, zh=zh, c=c, y=y, z=z):
        return (x * 4 + zh * 2 + c, y * NZ + z)

    def y_peer(k):
        return lax.rem(y + k, NY)

    def x_peer(k):
        return lax.rem(x + k, NX)

    loads = [
        pltpu.make_async_copy(src, dst, load_sem.at[i])
        for i, (src, dst) in enumerate(
            [(tok_hbm, tok), (cot_hbm, cot), (w_hbm, w), (shared_hbm, shared),
             (master_hbm, master), (mom_hbm, mom)]
        )
    ]
    for load in loads:
        load.start()

    barrier = pltpu.get_barrier_semaphore()

    def greet(where):
        pl.semaphore_signal(barrier, inc=1, device_id=where, device_id_type=MESH)

    for k in (1, 2, 3):
        greet(device(y=y_peer(k)))
        greet(device(x=x_peer(k)))
    greet(device(c=1 - c))
    greet(device(zh=1 - zh))

    @pl.when(z > 0)
    def _():
        greet(device(z=z - 1))

    @pl.when(z < NZ - 1)
    def _():
        greet(device(z=z + 1))

    def remote(src, dst, send, recv, where):
        return pltpu.make_async_remote_copy(
            src_ref=src, dst_ref=dst, send_sem=send, recv_sem=recv, device_id=where, device_id_type=MESH
        )

    def order(i):
        near = i // 2
        flip = lax.rem(i, 2) == jnp.where(z < NZ // 2, 0, 1)
        return jnp.where(flip, NZ - 1 - near, near)

    def my_rows():
        return pl.ds(pl.multiple_of(y * 128, 128), 128)

    def columns_of(peer, d):
        return pl.ds(pl.multiple_of((peer * NZ + d) * COLS, COLS), COLS)

    def token_copy(d, k):
        peer = y_peer(k)
        return remote(
            tok.at[:, columns_of(peer, d)], tokg.at[d, my_rows()], st.at[d, k - 1], rt.at[d, k - 1], device(y=peer)
        )

    def cot_copy(q, k):
        return remote(
            cotg.at[q, my_rows()], cotg.at[q, my_rows()], sc.at[q, k - 1], rc.at[q, k - 1], device(y=y_peer(k))
        )

    def send_tokens(d):
        for k in (1, 2, 3):
            token_copy(d, k).start()

    def wait_tokens(d):
        for k in (1, 2, 3):
            token_copy(d, k).wait_recv()

    loads[0].wait()
    pl.semaphore_wait(barrier, 8 + jnp.where(z > 0, 1, 0) + jnp.where(z < NZ - 1, 1, 0))
    send_tokens(order(0))

    def square(j, acc):
        t = tok[:, pl.ds(pl.multiple_of(j * 128, 128), 128)].astype(F32)
        return acc + t * t

    total = lax.fori_loop(0, 64, square, jnp.zeros((128, 128), F32), unroll=8)
    inverse = lax.rsqrt(jnp.sum(total, axis=1, keepdims=True) / 8192.0 + norm_eps)
    loads[1].wait()
    for q in range(SUBS):
        cotg[q, my_rows(), :] = (cot[:, q * COLS : (q + 1) * COLS].astype(F32) * inverse).astype(BF16)
        for k in (1, 2, 3):
            cot_copy(q, k).start()
    send_tokens(order(1))

    def keep(d, _):
        tokg[d, my_rows(), :] = tok[:, columns_of(y, d)]
        return 0

    lax.fori_loop(0, NZ, keep, 0)

    loads[2].wait()
    loads[3].wait()
    low = lax.broadcasted_iota(jnp.int32, (256, 128), 1) < BLOCK

    def decode(t, _):
        at = pl.ds(pl.multiple_of(t * 128, 128), 128)
        delta = shared[:, at].astype(F32) - w[:, at].astype(F32)
        size = jnp.abs(delta)
        first = jnp.max(jnp.where(low, size, 0.0), axis=1, keepdims=True)
        second = jnp.max(jnp.where(low, 0.0, size), axis=1, keepdims=True)
        largest = jnp.where(low, first, second)
        scale = ((largest + 1e-06) / code_range).astype(BF16).astype(F32)
        coded = (delta / scale).astype(BF16).astype(F32)
        dec[t // 2, :, pl.ds(pl.multiple_of(lax.rem(t, 2) * 128, 128), 128)] = (coded * scale).astype(BF16)
        return 0

    lax.fori_loop(0, 8, decode, 0)

    def scatter_copy(k):
        peer = x_peer(k)
        return remote(dec.at[peer], x_in.at[k - 1], sx.at[k - 1], rx.at[k - 1], device(x=peer))

    for k in (1, 2, 3):
        scatter_copy(k).start()

    mine = pl.ds(pl.multiple_of(c * 128, 128), 128)
    other = pl.ds(pl.multiple_of((1 - c) * 128, 128), 128)
    my_lanes = pl.ds(pl.multiple_of(zh * 128, 128), 128)
    far_lanes = pl.ds(pl.multiple_of((1 - zh) * 128, 128), 128)
    core = device(c=1 - c)
    far = device(zh=1 - zh)
    core_sum = remote(core_out, core_in, ss.at[0], rs.at[0], core)
    z_sum = remote(z_out, z_in, ss.at[1], rs.at[1], far)
    core_full = remote(full.at[mine], full.at[mine], ss.at[2], rs.at[2], core)
    core_pair = remote(pair_out, pair_in, ss.at[3], rs.at[3], core)
    z_gather = remote(sh.at[x, mine, my_lanes], sh.at[x, mine, my_lanes], ss.at[4], rs.at[4], far)
    core_gather = remote(sh.at[:, mine], sh_in, ss.at[5], rs.at[5], core)

    def gather_copy(k):
        return remote(sh.at[x, mine], sh.at[x, mine], sg.at[k - 1], rg.at[k - 1], device(x=x_peer(k)))

    def stage_x():
        for k in (1, 2, 3):
            scatter_copy(k).wait_recv()

        def summed(rows):
            acc = dec[x, rows, :].astype(F32)
            for k in range(3):
                acc = acc + x_in[k, rows, :].astype(F32)
            return acc

        core_out[...] = summed(other).astype(BF16)
        core_sum.start()
        half[...] = summed(mine)

    def stage_core():
        core_sum.wait_recv()
        half[...] = half[...] + core_in[...].astype(F32)
        z_out[...] = half[:, far_lanes].astype(BF16)
        z_sum.start()

    def stage_far():
        z_sum.wait_recv()
        full[mine, :] = half[:, my_lanes] + z_in[...].astype(F32)
        core_full.start()

    def stage_update():
        core_full.wait_recv()
        loads[4].wait()
        loads[5].wait()
        average = full[...] / float(REPLICAS)
        average = jnp.where(c == 0, average[:, :BLOCK], average[:, BLOCK:])
        momentum_next = outer_beta * mom[...] + average
        master_next = master[...] - outer_rate * (average + outer_beta * momentum_next)
        mom_out[...] = momentum_next
        master_out[...] = master_next
        twice = jnp.concatenate([master_next, master_next], axis=1)
        lanes = lax.broadcasted_iota(jnp.int32, (256, 128), 1) // BLOCK
        pair_out[...] = jnp.where(lanes == c, twice, 0.0).astype(BF16)
        core_pair.start()

    def stage_pair():
        core_pair.wait_recv()
        sh[x, :, my_lanes] = pair_out[...] + pair_in[...]
        z_gather.start()

    def stage_gather():
        z_gather.wait_recv()
        for k in (1, 2, 3):
            gather_copy(k).start()

    def stage_last():
        for k in (1, 2, 3):
            gather_copy(k).wait_recv()
        core_gather.start()

    stages = {1: stage_x, 2: stage_core, 7: stage_far, 8: stage_update, 9: stage_pair, 15: stage_gather, 17: stage_last}

    def product(d, q):
        return lax.dot_general(tokg[d], cotg[q], (((0,), (0,)), ((), ())), preferred_element_type=F32)

    count_f = SUBS * (NZ - 1 - z)
    count_b = SUBS * z
    lag_f = jnp.where(z < NZ // 2, 0, 4 * z - 10)
    lag_b = jnp.where(z < NZ // 2, 18 - 4 * z, 0)

    def forward(u):
        s, q = u // SUBS, lax.rem(u, SUBS)
        return remote(buf_f.at[s, q], buf_f.at[s, q], sf.at[u], rf.at[u], device(z=z + 1))

    def backward(u):
        s, q = u // SUBS, lax.rem(u, SUBS)
        return remote(buf_b.at[s, q], buf_b.at[s, q], sb.at[u], rb.at[u], device(z=z - 1))

    def unit(u, d, first, buf, copy):
        s, q = u // SUBS, lax.rem(u, SUBS)

        @pl.when(q == 0)
        def _():
            wait_tokens(d)

        part = product(d, q)

        @pl.when(first)
        def _():
            buf[s, q] = part.astype(BF16)

        @pl.when(jnp.logical_not(first))
        def _():
            copy(u).wait_recv()
            buf[s, q] = (part + buf[s, q].astype(F32)).astype(BF16)

        @pl.when(u >= DEPTH)
        def _():
            copy(u - DEPTH).wait_send()

        copy(u).start()

    def step(u, _):
        @pl.when(u < SUBS)
        def _():
            for k in (1, 2, 3):
                cot_copy(u, k).wait_recv()

        uf = u - lag_f
        ub = u - lag_b

        @pl.when((uf >= 0) & (uf < count_f))
        def _():
            unit(uf, NZ - 1 - uf // SUBS, z == 0, buf_f, forward)

        @pl.when((ub >= 0) & (ub < count_b))
        def _():
            unit(ub, ub // SUBS, z == NZ - 1, buf_b, backward)

        @pl.when(u < NZ - 2)
        def _():
            send_tokens(order(u + 2))

        for at, stage in stages.items():
            pl.when(u == at)(stage)
        return 0

    lax.fori_loop(0, UNITS, step, 0)

    wait_tokens(z)
    core_gather.wait_recv()
    for q in range(SUBS):
        sh[q, other, :] = sh_in[q]
    row = lax.broadcasted_iota(jnp.int32, (64, 128), 0)
    gain = gain_ref[...].astype(F32)
    tall = [
        jnp.transpose(
            jnp.broadcast_to(
                jnp.sum(jnp.where(row == 2 * fs + h, gain, 0.0), axis=0, keepdims=True), (128, 128)
            )
        )
        for h in range(2)
    ]
    tall = jnp.concatenate(tall, axis=0)
    rate = tall[:, :1] * (mix_weight * inner_gain / math.sqrt(32 * 128))
    for q in range(SUBS):
        full_sum = product(z, q)
        half_w = mix_weight * w[:, q * COLS : (q + 1) * COLS].astype(F32) + (1.0 - mix_weight) * sh[q].astype(F32)

        @pl.when(z > 0)
        def _():
            forward((NZ - 1 - z) * SUBS + q).wait_recv()

        @pl.when(z < NZ - 1)
        def _():
            backward(z * SUBS + q).wait_recv()

        near_f = jnp.minimum(NZ - 1 - z, NZ - 2)
        near_b = jnp.minimum(z, NZ - 2)
        left = jnp.where(z > 0, buf_f[near_f, q].astype(F32), 0.0)
        right = jnp.where(z < NZ - 1, buf_b[near_b, q].astype(F32), 0.0)
        layer_out[:, q * COLS : (q + 1) * COLS] = (half_w - rate * (full_sum + left + right)).astype(BF16)

    for k in (1, 2, 3):
        for d in range(NZ):
            token_copy(d, k).wait_send()
        for q in range(SUBS):
            cot_copy(q, k).wait_send()
        scatter_copy(k).wait_send()
        gather_copy(k).wait_send()
    for copy in (core_sum, z_sum, core_full, core_pair, z_gather, core_gather):
        copy.wait_send()

    @pl.when(z < NZ - 1)
    def _():
        for back in range(DEPTH):
            forward(count_f - 1 - back).wait_send()

    @pl.when(z > 0)
    def _():
        for back in range(DEPTH):
            backward(count_b - 1 - back).wait_send()


def on_device(tokens, norm_gain, cotangent, layer_weight, shared_copy, master, momentum):
    vmem, hbm = pltpu.VMEM, pl.ANY
    dma = pltpu.SemaphoreType.DMA
    scratch = [
        vmem((128, 8192), BF16), vmem((128, 1024), BF16), vmem((256, 1024), BF16), vmem((256, 1024), BF16),
        vmem((256, 64), F32), vmem((256, 64), F32),
        vmem((NZ, 512, COLS), BF16), vmem((SUBS, 512, COLS), BF16),
        vmem((NZ - 1, SUBS, 256, COLS), BF16), vmem((NZ - 1, SUBS, 256, COLS), BF16),
        vmem((4, 256, 256), BF16), vmem((3, 256, 256), BF16), vmem((128, 256), F32),
        vmem((128, 256), BF16), vmem((128, 256), BF16), vmem((128, 128), BF16), vmem((128, 128), BF16),
        vmem((256, 128), F32), vmem((256, 128), BF16), vmem((256, 128), BF16),
        vmem((4, 256, 256), BF16), vmem((4, 128, 256), BF16),
        dma((6,)),
        dma((NZ, 3)), dma((NZ, 3)), dma((SUBS, 3)), dma((SUBS, 3)),
        dma((UNITS,)), dma((UNITS,)), dma((UNITS,)), dma((UNITS,)),
        dma((3,)), dma((3,)), dma((3,)), dma((3,)), dma((6,)), dma((6,)),
    ]
    layer_next, master_next, momentum_next = pl.pallas_call(
        kernel,
        out_shape=[
            jax.ShapeDtypeStruct((256, 1024), BF16),
            jax.ShapeDtypeStruct((256, 64), F32),
            jax.ShapeDtypeStruct((256, 64), F32),
        ],
        in_specs=[pl.BlockSpec(memory_space=hbm), pl.BlockSpec(memory_space=vmem)]
        + [pl.BlockSpec(memory_space=hbm)] * 5,
        out_specs=[pl.BlockSpec(memory_space=vmem)] * 3,
        scratch_shapes=scratch,
        name="diloco_step",
        cost_estimate=pl.CostEstimate(flops=2 * 4096 * 256 * 1024, bytes_accessed=5 << 20, transcendentals=0),
        compiler_params=pltpu.CompilerParams(
            collective_id=0, has_side_effects=True, vmem_limit_bytes=48 << 20
        ),
    )(
        tokens[0], norm_gain.reshape(64, 128), cotangent[0], layer_weight[0], shared_copy, master, momentum
    )
    return (layer_next[None], master_next, momentum_next)


def solution(mesh):
    in_specs = (
        P("replica", "fsdp", None),
        P(),
        P("replica", "fsdp", None),
        P("replica", "fsdp", None),
        P("fsdp", None),
        P("fsdp", "replica"),
        P("fsdp", "replica"),
    )
    out_specs = (P("replica", "fsdp", None), P("fsdp", "replica"), P("fsdp", "replica"))
    return jax.shard_map(
        on_device, mesh=mesh, in_specs=in_specs, out_specs=out_specs, check_vma=False
    )
```

```python
import functools
import math

import jax
import jax.numpy as jnp
from jax import lax
from jax.experimental import pallas as pl
from jax.experimental.pallas import tpu as pltpu
from jax.sharding import PartitionSpec as P

BLOCK = 64
norm_eps = 1e-05
inner_gain = 0.4
outer_rate = 0.7
outer_beta = 0.9
mix_weight = 0.5
code_range = 448.0

NX, NY, NZ = 4, 4, 8
REPLICAS = 16
MESH = pl.DeviceIdType.MESH
F32, BF16 = jnp.float32, jnp.bfloat16
COLS = 256
SUBS = 4
UNITS = (NZ - 1) * SUBS
DEPTH = 3


def kernel(
    tok_hbm, gain_ref, cot_hbm, w_hbm, shared_hbm, master_hbm, mom_hbm,
    layer_out, master_out, mom_out,
    tok, cot, w, shared, master, mom, layer, master_new, mom_new,
    tokg, cotg, buf, acc, tok_edge, cot_edge, dec, x_in, half, core_out, core_in, z_out, z_in,
    full, pair_out, pair_in, sh, sh_in,
    load_sem, st, rt, sc, rc, su, ru, ste, rte, sce, rce, sye, rye, sx, rx, sg, rg, ss, rs, out_sem, wave_up, wave_down,
):
    rep, fs = lax.axis_index("replica"), lax.axis_index("fsdp")
    x, zh, c = rep // 4, lax.rem(rep // 2, 2), lax.rem(rep, 2)
    y, z = fs // NZ, lax.rem(fs, NZ)
    line = zh * NZ + z
    last = 2 * NZ - 1
    low_half = z < NZ // 2
    depth = jnp.where(low_half, z, NZ - 1 - z)
    inward = jnp.where(low_half, z + 1, z - 1)
    edge, second = depth == 0, depth == 1

    def device(x=x, zh=zh, c=c, y=y, z=z):
        return (x * 4 + zh * 2 + c, y * NZ + z)

    def on_line(at):
        return device(zh=at // NZ, z=lax.rem(at, NZ))

    def y_peer(k):
        return lax.rem(y + k, NY)

    def x_peer(k):
        return lax.rem(x + k, NX)

    loads = [
        pltpu.make_async_copy(src, dst, load_sem.at[i])
        for i, (src, dst) in enumerate(
            [(tok_hbm, tok), (cot_hbm, cot), (w_hbm, w), (shared_hbm, shared),
             (master_hbm, master), (mom_hbm, mom)]
        )
    ]
    loads[0].start()
    loads[1].start()
    barrier = pltpu.get_barrier_semaphore()

    def greet(where):
        pl.semaphore_signal(barrier, inc=1, device_id=where, device_id_type=MESH)

    for k in (1, 2, 3):
        greet(device(y=y_peer(k)))
        greet(device(x=x_peer(k)))
    greet(device(c=1 - c))

    @pl.when(line > 0)
    def _():
        greet(on_line(line - 1))

    @pl.when(line < last)
    def _():
        greet(on_line(line + 1))

    def remote(src, dst, send, recv, where):
        return pltpu.make_async_remote_copy(
            src_ref=src, dst_ref=dst, send_sem=send, recv_sem=recv, device_id=where, device_id_type=MESH
        )

    def dest(s):
        return jnp.where(low_half, NZ - 1 - s, s)

    def order(i):
        return jnp.where(lax.rem(i, 2) == 0, 1 + i // 2, NZ - 1 - (i - 3) // 2)

    def my_rows():
        return pl.ds(pl.multiple_of(y * 128, 128), 128)

    def columns_of(peer, d):
        return pl.ds(pl.multiple_of((peer * NZ + d) * COLS, COLS), COLS)

    def token_copy(d, k):
        peer = y_peer(k)
        return remote(
            tok.at[:, columns_of(peer, d)], tokg.at[d, my_rows()], st.at[d, k - 1], rt.at[d, k - 1], device(y=peer)
        )

    def cot_copy(q, k):
        return remote(
            cotg.at[q, my_rows()], cotg.at[q, my_rows()], sc.at[q, k - 1], rc.at[q, k - 1], device(y=y_peer(k))
        )

    def send_tokens(d):
        for k in (1, 2, 3):
            token_copy(d, k).start()

    def wait_tokens(d):
        for k in (1, 2, 3):
            token_copy(d, k).wait_recv()

    loads[0].wait()
    pl.semaphore_wait(barrier, 7 + jnp.where(line > 0, 1, 0) + jnp.where(line < last, 1, 0))
    send_tokens(dest(0))
    for load in loads[2:]:
        load.start()

    def square(j, acc):
        t = tok[:, pl.ds(pl.multiple_of(j * 128, 128), 128)].astype(F32)
        return acc + t * t

    total = lax.fori_loop(0, 64, square, jnp.zeros((128, 128), F32), unroll=8)
    inverse = lax.rsqrt(jnp.sum(total, axis=1, keepdims=True) / 8192.0 + norm_eps)
    loads[1].wait()
    for q in range(SUBS):
        cotg[q, my_rows(), :] = (cot[:, q * COLS : (q + 1) * COLS].astype(F32) * inverse).astype(BF16)
        for k in (1, 2, 3):
            cot_copy(q, k).start()
    send_tokens(dest(1))

    def edge_cot(q):
        return remote(
            cotg.at[q, my_rows()], cot_edge.at[q, my_rows()], sce.at[q], rce.at[q], device(z=inward)
        )

    def edge_relay(q, k):
        return remote(
            cot_edge.at[q, my_rows()], cot_edge.at[q, my_rows()], sye.at[q, k - 1], rye.at[q, k - 1],
            device(y=y_peer(k)),
        )

    def edge_tokens(s):
        return remote(tokg.at[dest(s)], tok_edge.at[s - 1], ste.at[s - 1], rte.at[s - 1], device(z=inward))

    @pl.when(edge)
    def _():
        for q in range(SUBS):
            edge_cot(q).start()

    def pass_up():
        @pl.when(line > 0)
        def _():
            pl.semaphore_wait(wave_up, 1)

        @pl.when(line < last)
        def _():
            pl.semaphore_signal(wave_up, inc=1, device_id=on_line(line + 1), device_id_type=MESH)

    def pass_down():
        @pl.when(line < last)
        def _():
            pl.semaphore_wait(wave_down, 1)

        @pl.when(line > 0)
        def _():
            pl.semaphore_signal(wave_down, inc=1, device_id=on_line(line - 1), device_id_type=MESH)

    def keep(d, _):
        tokg[d, my_rows(), :] = tok[:, columns_of(y, d)]
        return 0

    lax.fori_loop(0, NZ, keep, 0)

    loads[2].wait()
    loads[3].wait()
    low = lax.broadcasted_iota(jnp.int32, (256, 128), 1) < BLOCK

    def decode(t, _):
        at = pl.ds(pl.multiple_of(t * 128, 128), 128)
        delta = shared[:, at].astype(F32) - w[:, at].astype(F32)
        size = jnp.abs(delta)
        first = jnp.max(jnp.where(low, size, 0.0), axis=1, keepdims=True)
        second = jnp.max(jnp.where(low, 0.0, size), axis=1, keepdims=True)
        largest = jnp.where(low, first, second)
        scale = ((largest + 1e-06) / code_range).astype(BF16).astype(F32)
        coded = (delta / scale).astype(BF16).astype(F32)
        dec[t // 2, :, pl.ds(pl.multiple_of(lax.rem(t, 2) * 128, 128), 128)] = (coded * scale).astype(BF16)
        return 0

    lax.fori_loop(0, 8, decode, 0)

    def scatter_copy(k):
        peer = x_peer(k)
        return remote(dec.at[peer], x_in.at[k - 1], sx.at[k - 1], rx.at[k - 1], device(x=peer))

    for k in (1, 2, 3):
        scatter_copy(k).start()

    near_half = zh == 0
    pl.when(near_half)(pass_up)

    @pl.when(second)
    def _():
        for q in range(SUBS):
            edge_cot(q).wait_recv()
            for k in (1, 2, 3):
                edge_relay(q, k).start()

    mine = pl.ds(pl.multiple_of(c * 128, 128), 128)
    other = pl.ds(pl.multiple_of((1 - c) * 128, 128), 128)
    my_lanes = pl.ds(pl.multiple_of(zh * 128, 128), 128)
    far_lanes = pl.ds(pl.multiple_of((1 - zh) * 128, 128), 128)
    core = device(c=1 - c)
    far = device(zh=1 - zh)
    core_sum = remote(core_out, core_in, ss.at[0], rs.at[0], core)
    z_sum = remote(z_out, z_in, ss.at[1], rs.at[1], far)
    core_full = remote(full.at[mine], full.at[mine], ss.at[2], rs.at[2], core)
    core_pair = remote(pair_out, pair_in, ss.at[3], rs.at[3], core)
    z_gather = remote(sh.at[x, mine, my_lanes], sh.at[x, mine, my_lanes], ss.at[4], rs.at[4], far)
    core_gather = remote(sh.at[:, mine], sh_in, ss.at[5], rs.at[5], core)

    def gather_copy(k):
        return remote(sh.at[x, mine], sh.at[x, mine], sg.at[k - 1], rg.at[k - 1], device(x=x_peer(k)))

    stores = [
        pltpu.make_async_copy(src, dst, out_sem.at[i])
        for i, (src, dst) in enumerate([(master_new, master_out), (mom_new, mom_out)])
    ]

    def stage_x():
        for k in (1, 2, 3):
            scatter_copy(k).wait_recv()

        def summed(rows):
            acc = dec[x, rows, :].astype(F32)
            for k in range(3):
                acc = acc + x_in[k, rows, :].astype(F32)
            return acc

        core_out[...] = summed(other).astype(BF16)
        core_sum.start()
        half[...] = summed(mine)

    def stage_core():
        core_sum.wait_recv()
        half[...] = half[...] + core_in[...].astype(F32)
        z_out[...] = half[:, far_lanes].astype(BF16)
        z_sum.start()

    def stage_far():
        z_sum.wait_recv()
        full[mine, :] = half[:, my_lanes] + z_in[...].astype(F32)
        core_full.start()

    def stage_update():
        core_full.wait_recv()
        loads[4].wait()
        loads[5].wait()
        average = jnp.transpose(full[...]) / float(REPLICAS)
        average = jnp.where(c == 0, average[:BLOCK], average[BLOCK:])
        momentum_next = outer_beta * mom[...] + average
        master_next = master[...] - outer_rate * (average + outer_beta * momentum_next)
        mom_new[...] = momentum_next
        master_new[...] = master_next
        stores[0].start()
        stores[1].start()
        twice = jnp.concatenate([master_next, master_next], axis=0)
        share = lax.broadcasted_iota(jnp.int32, (128, 256), 0) // BLOCK
        pair_out[...] = jnp.transpose(jnp.where(share == c, twice, 0.0)).astype(BF16)
        core_pair.start()

    def stage_pair():
        core_pair.wait_recv()
        sh[x, :, my_lanes] = pair_out[...] + pair_in[...]
        z_gather.start()

    def stage_gather():
        z_gather.wait_recv()
        for k in (1, 2, 3):
            gather_copy(k).start()

    def stage_last():
        for k in (1, 2, 3):
            gather_copy(k).wait_recv()
        core_gather.start()

    def pick(*choices):
        at = choices[-1]
        for i in range(len(choices) - 1):
            at = jnp.where(depth == i, choices[i], at)
        return at

    up_at = jnp.where(z < 5, 0, jnp.where(z == 5, 2, jnp.where(z == 6, 4, 9)))
    down_far = jnp.where(z > 2, 0, jnp.where(z == 2, 2, jnp.where(z == 1, 4, 9)))
    down_near = jnp.where(low_half, pick(14, 9, 7, 5), pick(10, 6, 5, 4))
    core_at = jnp.where(near_half, down_near, jnp.maximum(up_at, 2))
    far_at = pick(15, 11, 10, 9)
    gather_at = jnp.where(near_half, pick(21, 21, 20, 19), pick(19, 16, 16, 16))
    stages = [
        (1, stage_x),
        (up_at, lambda: pl.when(jnp.logical_not(near_half))(pass_up)),
        (jnp.where(near_half, down_near, down_far), pass_down),
        (core_at, stage_core),
        (far_at, stage_far),
        (far_at + 1, stage_update),
        (far_at + 2, stage_pair),
        (gather_at, stage_gather),
        (gather_at + 2, stage_last),
    ]

    def multiply(rows, q):
        return lax.dot_general(rows, q, (((0,), (0,)), ((), ())), preferred_element_type=F32)

    def stream(way, u):
        s, q = u // SUBS, lax.rem(u, SUBS)
        to = jnp.where(way == 0, z + 1, z - 1)
        return remote(buf.at[way, s, q], buf.at[way, s, q], su.at[way, u], ru.at[way, u], device(z=to))

    count_in = jnp.where(edge, SUBS, SUBS * (NZ - 1 - depth))
    count_out = SUBS * depth
    inner = jnp.where(low_half, 0, 1)

    def unit(k, u):
        way = jnp.where(k == 0, inner, 1 - inner)
        v = jnp.where(k == 0, u, u - (18 - 4 * depth))

        @pl.when((v >= 0) & (v < jnp.where(k == 0, count_in, count_out)))
        def _():
            s, q = v // SUBS, lax.rem(v, SUBS)
            d = jnp.where(way == 0, NZ - 1 - s, s)
            joined = (k == 0) & second & (s > 0)

            @pl.when(q == 0)
            def _():
                wait_tokens(d)

            acc[...] = multiply(tokg[d], cotg[q])

            @pl.when(joined)
            def _():
                @pl.when(q == 0)
                def _():
                    edge_tokens(s).wait_recv()

                @pl.when(s == 1)
                def _():
                    for peer in (1, 2, 3):
                        edge_relay(q, peer).wait_recv()

                acc[...] += multiply(tok_edge[s - 1], cot_edge[q])

            @pl.when(jnp.logical_not(joined | (edge & (k == 0))))
            def _():
                stream(way, v).wait_recv()
                acc[...] += buf[way, s, q].astype(F32)

            buf[way, s, q] = acc[...].astype(BF16)

            @pl.when(v >= DEPTH)
            def _():
                stream(way, v - DEPTH).wait_send()

            stream(way, v).start()

    def forward_tokens(u):
        s = (u - 4) // 2 + 1

        @pl.when(edge & (u >= 4) & (u <= 14) & (lax.rem(u, 2) == 0))
        def _():
            wait_tokens(dest(s))

            @pl.when(s >= 3)
            def _():
                edge_tokens(s - 2).wait_send()

            edge_tokens(s).start()

    def step(u, _):
        @pl.when(u < SUBS)
        def _():
            for k in (1, 2, 3):
                cot_copy(u, k).wait_recv()

        def both(k, _):
            unit(k, u)
            return 0

        lax.fori_loop(0, 2, both, 0)
        forward_tokens(u)

        @pl.when(u < NZ - 2)
        def _():
            send_tokens(dest(order(u + 2)))

        for at, stage in stages:
            pl.when(u == at)(stage)
        return 0

    lax.fori_loop(0, UNITS, step, 0)

    wait_tokens(z)
    core_gather.wait_recv()
    for q in range(SUBS):
        sh[q, other, :] = sh_in[q]
    row = lax.broadcasted_iota(jnp.int32, (64, 128), 0)
    gain = gain_ref[...].astype(F32)
    tall = [
        jnp.transpose(
            jnp.broadcast_to(
                jnp.sum(jnp.where(row == 2 * fs + h, gain, 0.0), axis=0, keepdims=True), (128, 128)
            )
        )
        for h in range(2)
    ]
    tall = jnp.concatenate(tall, axis=0)
    rate = tall[:, :1] * (mix_weight * inner_gain / math.sqrt(32 * 128))

    def layer_store(q):
        at = pl.ds(pl.multiple_of(q * COLS, COLS), COLS)
        return pltpu.make_async_copy(layer.at[:, at], layer_out.at[:, at], out_sem.at[2 + q])

    @pl.when(second)
    def _():
        edge_tokens(NZ - 2).wait_recv()

    def finish(q, _):
        at = pl.ds(pl.multiple_of(q * COLS, COLS), COLS)
        acc[...] = multiply(tokg[z], cotg[q])

        @pl.when(second)
        def _():
            acc[...] += multiply(tok_edge[NZ - 3], cot_edge[q])

        @pl.when(z > 1)
        def _():
            stream(0, (NZ - 1 - z) * SUBS + q).wait_recv()
            acc[...] += buf[0, NZ - 1 - z, q].astype(F32)

        @pl.when(z < NZ - 2)
        def _():
            stream(1, z * SUBS + q).wait_recv()
            acc[...] += buf[1, z, q].astype(F32)

        half_w = mix_weight * w[:, at].astype(F32) + (1.0 - mix_weight) * sh[q].astype(F32)
        layer[:, at] = (half_w - rate * acc[...]).astype(BF16)
        layer_store(q).start()
        return 0

    lax.fori_loop(0, SUBS, finish, 0)

    for k in (1, 2, 3):
        for d in range(NZ):
            token_copy(d, k).wait_send()
        for q in range(SUBS):
            cot_copy(q, k).wait_send()
        scatter_copy(k).wait_send()
        gather_copy(k).wait_send()
    for copy in (core_sum, z_sum, core_full, core_pair, z_gather, core_gather):
        copy.wait_send()

    for store in stores + [layer_store(q) for q in range(SUBS)]:
        store.wait()

    for back in range(1, DEPTH + 1):
        stream(inner, count_in - back).wait_send()

    @pl.when(depth > 0)
    def _():
        for back in range(1, DEPTH + 1):
            stream(1 - inner, count_out - back).wait_send()

    @pl.when(edge)
    def _():
        for q in range(SUBS):
            edge_cot(q).wait_send()
        for s in (NZ - 3, NZ - 2):
            edge_tokens(s).wait_send()

    @pl.when(second)
    def _():
        for q in range(SUBS):
            for k in (1, 2, 3):
                edge_relay(q, k).wait_send()


def copy_kernel(*refs):
    for a, b in zip(refs[:3], refs[3:]):
        b[...] = a[...]


def on_device(tokens, norm_gain, cotangent, layer_weight, shared_copy, master, momentum):
    vmem, hbm = pltpu.VMEM, pl.ANY
    dma = pltpu.SemaphoreType.DMA
    scratch = [
        vmem((128, 8192), BF16), vmem((128, 1024), BF16), vmem((256, 1024), BF16), vmem((256, 1024), BF16),
        vmem((64, 256), F32), vmem((64, 256), F32),
        vmem((256, 1024), BF16), vmem((64, 256), F32), vmem((64, 256), F32),
        vmem((NZ, 512, COLS), BF16), vmem((SUBS, 512, COLS), BF16),
        vmem((2, NZ - 1, SUBS, 256, COLS), BF16), vmem((256, COLS), F32),
        vmem((NZ - 2, 512, COLS), BF16), vmem((SUBS, 512, COLS), BF16),
        vmem((4, 256, 256), BF16), vmem((3, 256, 256), BF16), vmem((128, 256), F32),
        vmem((128, 256), BF16), vmem((128, 256), BF16), vmem((128, 128), BF16), vmem((128, 128), BF16),
        vmem((256, 128), F32), vmem((256, 128), BF16), vmem((256, 128), BF16),
        vmem((4, 256, 256), BF16), vmem((4, 128, 256), BF16),
        dma((6,)),
        dma((NZ, 3)), dma((NZ, 3)), dma((SUBS, 3)), dma((SUBS, 3)),
        dma((2, UNITS)), dma((2, UNITS)),
        dma((NZ - 2,)), dma((NZ - 2,)), dma((SUBS,)), dma((SUBS,)), dma((SUBS, 3)), dma((SUBS, 3)),
        dma((3,)), dma((3,)), dma((3,)), dma((3,)), dma((6,)), dma((6,)),
        dma((6,)), pltpu.SemaphoreType.REGULAR, pltpu.SemaphoreType.REGULAR,
    ]
    layer_next, master_next, momentum_next = pl.pallas_call(
        kernel,
        out_shape=[
            jax.ShapeDtypeStruct((256, 1024), BF16),
            jax.ShapeDtypeStruct((64, 256), F32),
            jax.ShapeDtypeStruct((64, 256), F32),
        ],
        in_specs=[pl.BlockSpec(memory_space=hbm), pl.BlockSpec(memory_space=vmem)]
        + [pl.BlockSpec(memory_space=hbm)] * 5,
        out_specs=[pl.BlockSpec(memory_space=hbm)] * 3,
        scratch_shapes=scratch,
        name="diloco_step",
        cost_estimate=pl.CostEstimate(flops=2 * 4096 * 256 * 1024, bytes_accessed=5 << 20, transcendentals=0),
        compiler_params=pltpu.CompilerParams(
            collective_id=0, has_side_effects=True, vmem_limit_bytes=60 << 20
        ),
    )(
        tokens[0], norm_gain.reshape(64, 128), cotangent[0], layer_weight[0], shared_copy, master.T, momentum.T
    )
    results = (layer_next, master_next, momentum_next)
    layer_next, master_next, momentum_next = pl.pallas_call(
        copy_kernel,
        out_shape=[jax.ShapeDtypeStruct(r.shape, r.dtype) for r in results],
        in_specs=[pl.BlockSpec(memory_space=vmem)] * 3,
        out_specs=[pl.BlockSpec(memory_space=vmem)] * 3,
        name="write_out",
        compiler_params=pltpu.CompilerParams(vmem_limit_bytes=60 << 20),
    )(*results)
    return (layer_next[None], master_next.T, momentum_next.T)


def solution(mesh):
    in_specs = (
        P("replica", "fsdp", None),
        P(),
        P("replica", "fsdp", None),
        P("replica", "fsdp", None),
        P("fsdp", None),
        P("fsdp", "replica"),
        P("fsdp", "replica"),
    )
    out_specs = (P("replica", "fsdp", None), P("fsdp", "replica"), P("fsdp", "replica"))
    return jax.shard_map(
        on_device, mesh=mesh, in_specs=in_specs, out_specs=out_specs, check_vma=False
    )
```

```python
import functools
import math

import jax
import jax.numpy as jnp
from jax import lax
from jax.experimental import pallas as pl
from jax.experimental.pallas import tpu as pltpu
from jax.sharding import PartitionSpec as P

BLOCK = 64
norm_eps = 1e-05
inner_gain = 0.4
outer_rate = 0.7
outer_beta = 0.9
mix_weight = 0.5
code_range = 448.0

NX, NY, NZ = 4, 4, 8
REPLICAS = 16
MESH = pl.DeviceIdType.MESH
F32, BF16 = jnp.float32, jnp.bfloat16
COLS = 256
SUBS = 4
PARTS = 2 * SUBS
UNITS = (NZ - 1) * PARTS
DEPTH = 4


def kernel(
    tok_hbm, gain_ref, cot_hbm, w_hbm, shared_hbm, master_hbm, mom_hbm,
    layer_out, master_out, mom_out,
    tok, cot, w, shared, master, mom, layer, master_new, mom_new,
    tokg, cotg, buf, acc, own, rates, tok_edge, cot_edge, dec, x_in, half, core_out, core_in, z_out, z_in,
    full, pair_out, pair_in, sh, sh_in,
    load_sem, st, rt, sc, rc, su, ru, ste, rte, sce, rce, sye, rye, sx, rx, sg, rg, ss, rs, out_sem, wave_up, wave_down,
):
    rep, fs = lax.axis_index("replica"), lax.axis_index("fsdp")
    x, zh, c = rep // 4, lax.rem(rep // 2, 2), lax.rem(rep, 2)
    y, z = fs // NZ, lax.rem(fs, NZ)
    line = zh * NZ + z
    last = 2 * NZ - 1
    low_half = z < NZ // 2
    depth = jnp.where(low_half, z, NZ - 1 - z)
    inward = jnp.where(low_half, z + 1, z - 1)
    edge, second = depth == 0, depth == 1

    def device(x=x, zh=zh, c=c, y=y, z=z):
        return (x * 4 + zh * 2 + c, y * NZ + z)

    def on_line(at):
        return device(zh=at // NZ, z=lax.rem(at, NZ))

    def y_peer(k):
        return lax.rem(y + k, NY)

    def x_peer(k):
        return lax.rem(x + k, NX)

    loads = [
        pltpu.make_async_copy(src, dst, load_sem.at[i])
        for i, (src, dst) in enumerate(
            [(tok_hbm, tok), (cot_hbm, cot), (w_hbm, w), (shared_hbm, shared),
             (master_hbm, master), (mom_hbm, mom)]
        )
    ]
    loads[0].start()
    loads[1].start()
    barrier = pltpu.get_barrier_semaphore()

    def greet(where):
        pl.semaphore_signal(barrier, inc=1, device_id=where, device_id_type=MESH)

    for k in (1, 2, 3):
        greet(device(y=y_peer(k)))
        greet(device(x=x_peer(k)))
    greet(device(c=1 - c))

    @pl.when(line > 0)
    def _():
        greet(on_line(line - 1))

    @pl.when(line < last)
    def _():
        greet(on_line(line + 1))

    def remote(src, dst, send, recv, where):
        return pltpu.make_async_remote_copy(
            src_ref=src, dst_ref=dst, send_sem=send, recv_sem=recv, device_id=where, device_id_type=MESH
        )

    def dest(s):
        return jnp.where(low_half, NZ - 1 - s, s)

    def order(i):
        return jnp.where(lax.rem(i, 2) == 0, 1 + i // 2, NZ - 1 - (i - 3) // 2)

    def my_rows():
        return pl.ds(pl.multiple_of(y * 128, 128), 128)

    def columns_of(peer, d):
        return pl.ds(pl.multiple_of((peer * NZ + d) * COLS, COLS), COLS)

    def half_columns(peer, d, h):
        return pl.ds(pl.multiple_of((peer * NZ + d) * COLS + h * 128, 128), 128)

    def token_copy(d, k):
        peer = y_peer(k)
        return remote(tok.at[:, columns_of(peer, d)], tokg.at[d, my_rows()], st, rt.at[d], device(y=peer))

    def token_half(d, k, h):
        peer = y_peer(k)
        return remote(
            tok.at[:, half_columns(peer, d, h)], tokg.at[d, my_rows(), pl.ds(h * 128, 128)],
            st, rt.at[d if h == 0 else NZ], device(y=peer),
        )

    def cot_copy(q, k):
        return remote(cotg.at[q, my_rows()], cotg.at[q, my_rows()], sc, rc.at[q], device(y=y_peer(k)))

    def arrived(ref, sem):
        remote(ref, ref, st, sem, device(y=y_peer(1))).wait_recv()

    def departed(ref, sem):
        remote(ref, ref, sem, rt.at[0], device(y=y_peer(1))).wait_send()

    three = pl.ds(0, 3 * 128)

    def wait_half(h):
        d = dest(0)
        arrived(tokg.at[d, three, pl.ds(h * 128, 128)], rt.at[d if h == 0 else NZ])

    def send_tokens(d):
        for k in (1, 2, 3):
            token_copy(d, k).start()

    def wait_tokens(d):
        arrived(tokg.at[d, three], rt.at[d])

    def wait_cots(q):
        arrived(cotg.at[q, three], rc.at[q])

    loads[0].wait()
    pl.semaphore_wait(barrier, 7 + jnp.where(line > 0, 1, 0) + jnp.where(line < last, 1, 0))
    for k in (1, 2, 3):
        token_half(dest(0), k, 0).start()
    for load in loads[2:]:
        load.start()

    def square(j, acc):
        t = tok[:, pl.ds(pl.multiple_of(j * 128, 128), 128)].astype(F32)
        return acc + t * t

    total = lax.fori_loop(0, 64, square, jnp.zeros((128, 128), F32), unroll=8)
    inverse = lax.rsqrt(jnp.sum(total, axis=1, keepdims=True) / 8192.0 + norm_eps)
    loads[1].wait()
    for q in range(SUBS):
        cotg[q, my_rows(), :] = (cot[:, q * COLS : (q + 1) * COLS].astype(F32) * inverse).astype(BF16)
        for k in (1, 2, 3):
            cot_copy(q, k).start()
        if q == 0:
            for k in (1, 2, 3):
                token_half(dest(0), k, 1).start()

    def edge_cot(q):
        return remote(
            cotg.at[q, my_rows()], cot_edge.at[q, my_rows()], sce, rce, device(z=inward)
        )

    def edge_relay(q, k):
        return remote(
            cot_edge.at[q, my_rows()], cot_edge.at[q, my_rows()], sye, rye.at[q],
            device(y=y_peer(k)),
        )

    def edge_tokens(s, h):
        lanes = pl.ds(h * 128, 128)
        return remote(
            tokg.at[dest(s), :, lanes], tok_edge.at[s - 1, :, lanes],
            ste.at[lax.rem(s, 2)], rte.at[s - 1, h], device(z=inward),
        )

    @pl.when(edge)
    def _():
        for q in range(SUBS):
            edge_cot(q).start()

    def pass_up():
        @pl.when(line > 0)
        def _():
            pl.semaphore_wait(wave_up, 1)

        @pl.when(line < last)
        def _():
            pl.semaphore_signal(wave_up, inc=1, device_id=on_line(line + 1), device_id_type=MESH)

    def pass_down():
        @pl.when(line < last)
        def _():
            pl.semaphore_wait(wave_down, 1)

        @pl.when(line > 0)
        def _():
            pl.semaphore_signal(wave_down, inc=1, device_id=on_line(line - 1), device_id_type=MESH)

    def keep(d, _):
        tokg[d, my_rows(), :] = tok[:, columns_of(y, d)]
        return 0

    lax.fori_loop(0, NZ, keep, 0)

    loads[2].wait()
    loads[3].wait()
    low = lax.broadcasted_iota(jnp.int32, (256, 128), 1) < BLOCK

    def decode(t, _):
        at = pl.ds(pl.multiple_of(t * 128, 128), 128)
        delta = shared[:, at].astype(F32) - w[:, at].astype(F32)
        size = jnp.abs(delta)
        first = jnp.max(jnp.where(low, size, 0.0), axis=1, keepdims=True)
        second = jnp.max(jnp.where(low, 0.0, size), axis=1, keepdims=True)
        largest = jnp.where(low, first, second)
        scale = ((largest + 1e-06) / code_range).astype(BF16).astype(F32)
        coded = (delta / scale).astype(BF16).astype(F32)
        dec[t // 2, :, pl.ds(pl.multiple_of(lax.rem(t, 2) * 128, 128), 128)] = (coded * scale).astype(BF16)
        return 0

    lax.fori_loop(0, 8, decode, 0)

    def scatter_copy(k):
        peer = x_peer(k)
        return remote(dec.at[peer], x_in.at[k - 1], sx, rx, device(x=peer))

    for k in (1, 2, 3):
        scatter_copy(k).start()

    near_half = zh == 0
    pl.when(near_half)(pass_up)

    mine = pl.ds(pl.multiple_of(c * 128, 128), 128)
    other = pl.ds(pl.multiple_of((1 - c) * 128, 128), 128)
    my_lanes = pl.ds(pl.multiple_of(zh * 128, 128), 128)
    far_lanes = pl.ds(pl.multiple_of((1 - zh) * 128, 128), 128)
    core = device(c=1 - c)
    far = device(zh=1 - zh)
    core_sum = remote(core_out, core_in, ss, rs.at[0], core)
    z_sum = remote(z_out, z_in, ss, rs.at[1], far)
    core_full = remote(full.at[mine], full.at[mine], ss, rs.at[2], core)
    core_pair = remote(pair_out, pair_in, ss, rs.at[3], core)
    z_gather = remote(sh.at[x, mine, my_lanes], sh.at[x, mine, my_lanes], ss, rs.at[4], far)
    core_gather = remote(sh.at[:, mine], sh_in, ss, rs.at[5], core)

    def gather_copy(k):
        return remote(sh.at[x, mine], sh.at[x, mine], sg, rg, device(x=x_peer(k)))

    stores = [
        pltpu.make_async_copy(src, dst, out_sem.at[i])
        for i, (src, dst) in enumerate([(master_new, master_out), (mom_new, mom_out)])
    ]

    def stage_x():
        arrived(x_in, rx)

        def summed(rows):
            acc = dec[x, rows, :].astype(F32)
            for k in range(3):
                acc = acc + x_in[k, rows, :].astype(F32)
            return acc

        core_out[...] = summed(other).astype(BF16)
        core_sum.start()
        half[...] = summed(mine)

    def stage_core():
        core_sum.wait_recv()
        half[...] = half[...] + core_in[...].astype(F32)
        z_out[...] = half[:, far_lanes].astype(BF16)
        z_sum.start()

    def stage_far():
        z_sum.wait_recv()
        full[mine, :] = half[:, my_lanes] + z_in[...].astype(F32)
        core_full.start()

    def stage_update():
        core_full.wait_recv()
        loads[4].wait()
        loads[5].wait()
        average = jnp.transpose(full[...]) / float(REPLICAS)
        average = jnp.where(c == 0, average[:BLOCK], average[BLOCK:])
        momentum_next = outer_beta * mom[...] + average
        master_next = master[...] - outer_rate * (average + outer_beta * momentum_next)
        mom_new[...] = momentum_next
        master_new[...] = master_next
        stores[0].start()
        stores[1].start()
        twice = jnp.concatenate([master_next, master_next], axis=0)
        share = lax.broadcasted_iota(jnp.int32, (128, 256), 0) // BLOCK
        pair_out[...] = jnp.transpose(jnp.where(share == c, twice, 0.0)).astype(BF16)
        core_pair.start()

    def stage_pair():
        core_pair.wait_recv()
        sh[x, :, my_lanes] = pair_out[...] + pair_in[...]
        z_gather.start()

    def stage_gather():
        z_gather.wait_recv()
        for k in (1, 2, 3):
            gather_copy(k).start()

    def stage_last():
        arrived(sh_in.at[pl.ds(0, 3)], rg)
        core_gather.start()

    def pick(*choices):
        at = choices[-1]
        for i in range(len(choices) - 1):
            at = jnp.where(depth == i, choices[i], at)
        return at

    def by_place(low, high):
        return jnp.where(low_half, pick(*low), pick(*high))

    up_at = by_place((1, 1, 1, 1), (10, 8, 4, 1))
    down_far = by_place((10, 8, 4, 1), (1, 1, 1, 1))
    down_near = by_place((22, 20, 16, 10), (12, 12, 10, 8))
    core_at = jnp.where(near_half, down_near, jnp.maximum(up_at, 4))
    far_at = jnp.where(
        near_half, by_place((24, 23, 20, 18), (18, 18, 16, 16)), by_place((24, 23, 20, 17), (20, 20, 18, 17))
    )
    gather_at = jnp.where(near_half, by_place((42, 42, 38, 35), (36, 35, 34, 34)), pick(32, 32, 30, 29))
    stages = [
        (2, stage_x),
        (up_at, lambda: pl.when(jnp.logical_not(near_half))(pass_up)),
        (jnp.where(near_half, down_near, down_far), pass_down),
        (core_at, stage_core),
        (far_at, stage_far),
        (far_at + 2, stage_update),
        (far_at + 4, stage_pair),
        (gather_at, stage_gather),
        (gather_at + 4, stage_last),
    ]

    def multiply(rows, columns):
        return lax.dot_general(rows, columns, (((0,), (0,)), ((), ())), preferred_element_type=F32)

    def split(j, by_column):
        h = jnp.where(by_column, lax.rem(j, 2), lax.rem(j // 2, 2))
        q = jnp.where(by_column, j // 2, 2 * (j // SUBS) + lax.rem(j, 2))
        return pl.ds(pl.multiple_of(h * 128, 128), 128), q

    def stream(way, v):
        s, j = v // PARTS, lax.rem(v, PARTS)
        to = jnp.where(way == 0, z + 1, z - 1)
        slot = jnp.where(way == 0, v, NZ * PARTS + PARTS - 1 - v)
        return remote(
            buf.at[way, s, j], buf.at[way, s, j], su.at[way, lax.rem(v, DEPTH)], ru.at[slot], device(z=to)
        )

    count_in = jnp.where(edge, PARTS, PARTS * (NZ - 1 - depth))
    count_out = PARTS * depth
    inner = jnp.where(low_half, 0, 1)

    def wait_first(k, d, h):
        @pl.when(k == 0)
        def _():
            wait_half(h)

        if h == 0:
            pl.when(k == 1)(lambda: wait_tokens(d))

    def unit(k, u):
        way = jnp.where(k == 0, inner, 1 - inner)
        v = jnp.where(k == 0, u, u - (36 - 8 * depth))

        @pl.when((v >= 0) & (v < jnp.where(k == 0, count_in, count_out)))
        def _():
            s, j = v // PARTS, lax.rem(v, PARTS)
            d = jnp.where(way == 0, NZ - 1 - s, s)
            rows, q = split(j, s == 0)
            joined = (k == 0) & second & (s > 0)

            @pl.when(s == 0)
            def _():
                for h in range(2):
                    pl.when(j == h)(lambda: wait_first(k, d, h))

            @pl.when((s > 0) & (j == 0))
            def _():
                wait_tokens(d)

            acc[...] = multiply(tokg[d, :, rows], cotg[q])

            @pl.when(joined)
            def _():
                for h in range(2):
                    pl.when(j == 2 * h)(lambda: edge_tokens(s, h).wait_recv())

                @pl.when((s == 1) & (lax.rem(j // 2, 2) == 0))
                def _():
                    arrived(cot_edge.at[q, three], rye.at[q])

                acc[...] += multiply(tok_edge[s - 1, :, rows], cot_edge[q])

            @pl.when(jnp.logical_not(joined | (edge & (k == 0))))
            def _():
                stream(way, v).wait_recv()
                acc[...] += buf[way, s, j].astype(F32)

            buf[way, s, j] = acc[...].astype(BF16)

            @pl.when(v >= DEPTH)
            def _():
                stream(way, v - DEPTH).wait_send()

            stream(way, v).start()

    def forward_tokens(u):
        s = (u - PARTS) // 4 + 1

        @pl.when(edge & (u >= PARTS) & (s < NZ - 1) & (lax.rem(u, 4) == 0))
        def _():
            wait_tokens(dest(s))

            @pl.when(s >= 3)
            def _():
                departed(tokg.at[0], ste.at[lax.rem(s, 2)])

            for h in range(2):
                edge_tokens(s, h).start()

    relays = jnp.where(second, SUBS, 0)

    def y_job(u):
        i = u // 2

        @pl.when((lax.rem(u, 2) == 0) & (i <= NZ - 2 + relays))
        def _():
            pl.when(i == 0)(lambda: send_tokens(dest(1)))

            @pl.when((i > 0) & (i <= relays))
            def _():
                pl.when(i == 1)(lambda: arrived(cot_edge.at[:, my_rows()], rce))
                for k in (1, 2, 3):
                    edge_relay(i - 1, k).start()

            pl.when(i > relays)(lambda: send_tokens(dest(order(i - relays + 1))))

    def step(u, _):
        @pl.when((u < PARTS) & (lax.rem(u, 2) == 0))
        def _():
            wait_cots(u // 2)

        def both(k, _):
            unit(k, u)
            return 0

        lax.fori_loop(0, 2, both, 0)
        forward_tokens(u)

        y_job(u)
        for at, stage in stages:
            pl.when(u == at)(stage)
        return 0

    lax.fori_loop(0, UNITS, step, 0)

    wait_tokens(z)

    @pl.when(second)
    def _():
        for h in range(2):
            edge_tokens(NZ - 2, h).wait_recv()

    core_gather.wait_recv()
    for q in range(SUBS):
        sh[q, other, :] = sh_in[q]
    row = lax.broadcasted_iota(jnp.int32, (64, 128), 0)
    gain = gain_ref[...].astype(F32) * (mix_weight * inner_gain / math.sqrt(32 * 128))
    for h in range(2):
        line_gain = jnp.sum(jnp.where(row == 2 * fs + h, gain, 0.0), axis=0, keepdims=True)
        tall = jnp.transpose(jnp.broadcast_to(line_gain, (128, 128)))
        rates[pl.ds(h * 128, 128), :] = jnp.concatenate([tall, tall], axis=1)

    def prepare(j, _):
        rows, q = split(j, edge)
        at = pl.ds(pl.multiple_of(q * COLS, COLS), COLS)
        acc[...] = multiply(tokg[z, :, rows], cotg[q])

        @pl.when(second)
        def _():
            acc[...] += multiply(tok_edge[NZ - 3, :, rows], cot_edge[q])

        half_w = mix_weight * w[rows, at].astype(F32) + (1.0 - mix_weight) * sh[q, rows, :].astype(F32)
        own[j] = half_w - rates[rows, :] * acc[...]
        return 0

    lax.fori_loop(0, PARTS, prepare, 0)

    def finish(j, _):
        rows, q = split(j, edge)
        at = pl.ds(pl.multiple_of(q * COLS, COLS), COLS)

        @pl.when(z > 1)
        def _():
            stream(0, (NZ - 1 - z) * PARTS + j).wait_recv()
            own[j] -= rates[rows, :] * buf[0, NZ - 1 - z, j].astype(F32)

        @pl.when(z < NZ - 2)
        def _():
            stream(1, z * PARTS + j).wait_recv()
            own[j] -= rates[rows, :] * buf[1, z, j].astype(F32)

        layer[rows, at] = own[j].astype(BF16)
        pltpu.make_async_copy(layer.at[rows, at], layer_out.at[rows, at], out_sem.at[2]).start()
        return 0

    lax.fori_loop(0, PARTS, finish, 0)
    departed(tok.at[:, pl.ds(0, 6144)], st)
    departed(cotg.at[pl.ds(0, 3)], sc)
    departed(dec.at[pl.ds(0, 3)], sx)
    departed(sh_in.at[pl.ds(0, 3)], sg)
    departed(dec, ss)
    for store in stores:
        store.wait()
    pltpu.make_async_copy(layer, layer_out, out_sem.at[2]).wait()

    for back in range(1, DEPTH + 1):
        stream(inner, count_in - back).wait_send()

    @pl.when(depth > 0)
    def _():
        for back in range(1, DEPTH + 1):
            stream(1 - inner, count_out - back).wait_send()

    @pl.when(edge)
    def _():
        departed(cotg.at[0], sce)
        for s in range(2):
            departed(tokg.at[0], ste.at[s])

    @pl.when(second)
    def _():
        departed(cot_edge.at[pl.ds(0, 3)], sye)


def copy_kernel(*refs):
    for a, b in zip(refs[:3], refs[3:]):
        b[...] = a[...]


def on_device(tokens, norm_gain, cotangent, layer_weight, shared_copy, master, momentum):
    vmem, hbm = pltpu.VMEM, pl.ANY
    dma = pltpu.SemaphoreType.DMA
    scratch = [
        vmem((128, 8192), BF16), vmem((128, 1024), BF16), vmem((256, 1024), BF16), vmem((256, 1024), BF16),
        vmem((64, 256), F32), vmem((64, 256), F32),
        vmem((256, 1024), BF16), vmem((64, 256), F32), vmem((64, 256), F32),
        vmem((NZ, 512, COLS), BF16), vmem((SUBS, 512, COLS), BF16),
        vmem((2, NZ - 1, PARTS, 128, COLS), BF16), vmem((128, COLS), F32),
        vmem((PARTS, 128, COLS), F32), vmem((256, COLS), F32),
        vmem((NZ - 2, 512, COLS), BF16), vmem((SUBS, 512, COLS), BF16),
        vmem((4, 256, 256), BF16), vmem((3, 256, 256), BF16), vmem((128, 256), F32),
        vmem((128, 256), BF16), vmem((128, 256), BF16), vmem((128, 128), BF16), vmem((128, 128), BF16),
        vmem((256, 128), F32), vmem((256, 128), BF16), vmem((256, 128), BF16),
        vmem((4, 256, 256), BF16), vmem((4, 128, 256), BF16),
        dma((6,)), dma, dma((NZ + 1,)), dma, dma((SUBS,)),
        dma((2, DEPTH)), dma(((NZ + 1) * PARTS,)),
        dma((2,)), dma((NZ - 2, 2)), dma, dma, dma, dma((SUBS,)),
        dma, dma, dma, dma, dma, dma((6,)), dma((3,)),
        pltpu.SemaphoreType.REGULAR, pltpu.SemaphoreType.REGULAR,
    ]
    layer_next, master_next, momentum_next = pl.pallas_call(
        kernel,
        out_shape=[
            jax.ShapeDtypeStruct((256, 1024), BF16),
            jax.ShapeDtypeStruct((64, 256), F32),
            jax.ShapeDtypeStruct((64, 256), F32),
        ],
        in_specs=[pl.BlockSpec(memory_space=hbm), pl.BlockSpec(memory_space=vmem)]
        + [pl.BlockSpec(memory_space=hbm)] * 5,
        out_specs=[pl.BlockSpec(memory_space=hbm)] * 3,
        scratch_shapes=scratch,
        name="diloco_step",
        cost_estimate=pl.CostEstimate(flops=2 * 4096 * 256 * 1024, bytes_accessed=5 << 20, transcendentals=0),
        compiler_params=pltpu.CompilerParams(
            collective_id=0, has_side_effects=True, vmem_limit_bytes=60 << 20
        ),
    )(
        tokens[0], norm_gain.reshape(64, 128), cotangent[0], layer_weight[0], shared_copy, master.T, momentum.T
    )
    results = (layer_next, master_next, momentum_next)
    layer_next, master_next, momentum_next = pl.pallas_call(
        copy_kernel,
        out_shape=[jax.ShapeDtypeStruct(r.shape, r.dtype) for r in results],
        in_specs=[pl.BlockSpec(memory_space=vmem)] * 3,
        out_specs=[pl.BlockSpec(memory_space=vmem)] * 3,
        name="write_out",
        compiler_params=pltpu.CompilerParams(vmem_limit_bytes=60 << 20),
    )(*results)
    return (layer_next[None], master_next.T, momentum_next.T)


def solution(mesh):
    in_specs = (
        P("replica", "fsdp", None),
        P(),
        P("replica", "fsdp", None),
        P("replica", "fsdp", None),
        P("fsdp", None),
        P("fsdp", "replica"),
        P("fsdp", "replica"),
    )
    out_specs = (P("replica", "fsdp", None), P("fsdp", "replica"), P("fsdp", "replica"))
    return jax.shard_map(
        on_device, mesh=mesh, in_specs=in_specs, out_specs=out_specs, check_vma=False
    )
```

```python
import functools
import math

import jax
import jax.numpy as jnp
from jax import lax
from jax.experimental import pallas as pl
from jax.experimental.pallas import tpu as pltpu
from jax.sharding import PartitionSpec as P

BLOCK = 64
norm_eps = 1e-05
inner_gain = 0.4
outer_rate = 0.7
outer_beta = 0.9
mix_weight = 0.5
code_range = 448.0

NX, NY, NZ = 4, 4, 8
REPLICAS = 16
MESH = pl.DeviceIdType.MESH
F32, BF16 = jnp.float32, jnp.bfloat16
COLS = 256
SUBS = 4
PARTS = 2 * SUBS
UNITS = (NZ - 1) * PARTS
DEPTH = 8


def kernel(
    tok_hbm, gain_ref, cot_hbm, w_hbm, shared_hbm, master_hbm, mom_hbm,
    layer_out, master_out, mom_out,
    tok, cot, w, shared, master, mom, layer, master_new, mom_new,
    tokg, cotg, buf, acc, own, rates, tok_edge, cot_edge, dec, x_in, half, core_out, core_in, z_out, z_in,
    full, pair_out, pair_in, sh, sh_in,
    load_sem, st, rt, sc, rc, su, ru, ste, rte, sce, rce, sye, rye, sx, rx, sg, rg, ss, rs, out_sem, wave_up, wave_down,
):
    rep, fs = lax.axis_index("replica"), lax.axis_index("fsdp")
    x, zh, c = rep // 4, lax.rem(rep // 2, 2), lax.rem(rep, 2)
    y, z = fs // NZ, lax.rem(fs, NZ)
    line = zh * NZ + z
    last = 2 * NZ - 1
    low_half = z < NZ // 2
    depth = jnp.where(low_half, z, NZ - 1 - z)
    inward = jnp.where(low_half, z + 1, z - 1)
    edge, second = depth == 0, depth == 1

    def device(x=x, zh=zh, c=c, y=y, z=z):
        return (x * 4 + zh * 2 + c, y * NZ + z)

    def on_line(at):
        return device(zh=at // NZ, z=lax.rem(at, NZ))

    def y_peer(k):
        return lax.rem(y + k, NY)

    def x_peer(k):
        return lax.rem(x + k, NX)

    loads = [
        pltpu.make_async_copy(src, dst, load_sem.at[i])
        for i, (src, dst) in enumerate(
            [(tok_hbm, tok), (cot_hbm, cot), (w_hbm, w), (shared_hbm, shared),
             (master_hbm, master), (mom_hbm, mom)]
        )
    ]
    loads[0].start()
    loads[1].start()
    barrier = pltpu.get_barrier_semaphore()

    def greet(where):
        pl.semaphore_signal(barrier, inc=1, device_id=where, device_id_type=MESH)

    for k in (1, 2, 3):
        greet(device(y=y_peer(k)))
        greet(device(x=x_peer(k)))
    greet(device(c=1 - c))

    @pl.when(line > 0)
    def _():
        greet(on_line(line - 1))

    @pl.when(line < last)
    def _():
        greet(on_line(line + 1))

    def remote(src, dst, send, recv, where):
        return pltpu.make_async_remote_copy(
            src_ref=src, dst_ref=dst, send_sem=send, recv_sem=recv, device_id=where, device_id_type=MESH
        )

    def dest(s):
        return jnp.where(low_half, NZ - 1 - s, s)

    def order(i):
        return jnp.where(lax.rem(i, 2) == 0, 1 + i // 2, NZ - 1 - (i - 3) // 2)

    def my_rows():
        return pl.ds(pl.multiple_of(y * 128, 128), 128)

    def columns_of(peer, d):
        return pl.ds(pl.multiple_of((peer * NZ + d) * COLS, COLS), COLS)

    def half_columns(peer, d, h):
        return pl.ds(pl.multiple_of((peer * NZ + d) * COLS + h * 128, 128), 128)

    def token_copy(d, k):
        peer = y_peer(k)
        return remote(tok.at[:, columns_of(peer, d)], tokg.at[d, my_rows()], st, rt.at[d], device(y=peer))

    def token_half(d, k, h):
        peer = y_peer(k)
        return remote(
            tok.at[:, half_columns(peer, d, h)], tokg.at[d, my_rows(), pl.ds(h * 128, 128)],
            st, rt.at[d if h == 0 else NZ], device(y=peer),
        )

    def cot_copy(q, k):
        return remote(cotg.at[q, my_rows()], cotg.at[q, my_rows()], sc, rc.at[q], device(y=y_peer(k)))

    def arrived(ref, sem):
        remote(ref, ref, st, sem, device(y=y_peer(1))).wait_recv()

    def departed(ref, sem):
        remote(ref, ref, sem, rt.at[0], device(y=y_peer(1))).wait_send()

    three = pl.ds(0, 3 * 128)

    def wait_half(h):
        d = dest(0)
        arrived(tokg.at[d, three, pl.ds(h * 128, 128)], rt.at[d if h == 0 else NZ])

    def send_tokens(d):
        for k in (1, 2, 3):
            token_copy(d, k).start()

    def wait_tokens(d):
        arrived(tokg.at[d, three], rt.at[d])

    def wait_cots(q):
        arrived(cotg.at[q, three], rc.at[q])

    loads[0].wait()
    pl.semaphore_wait(barrier, 7 + jnp.where(line > 0, 1, 0) + jnp.where(line < last, 1, 0))
    for k in (1, 2, 3):
        token_half(dest(0), k, 0).start()
    for load in loads[2:]:
        load.start()

    def square(j, acc):
        t = tok[:, pl.ds(pl.multiple_of(j * 128, 128), 128)].astype(F32)
        return acc + t * t

    total = lax.fori_loop(0, 64, square, jnp.zeros((128, 128), F32), unroll=8)
    inverse = lax.rsqrt(jnp.sum(total, axis=1, keepdims=True) / 8192.0 + norm_eps)
    loads[1].wait()
    for q in range(SUBS):
        cotg[q, my_rows(), :] = (cot[:, q * COLS : (q + 1) * COLS].astype(F32) * inverse).astype(BF16)
        if q == 0:
            for k in (1, 2, 3):
                cot_copy(q, k).start()
            for k in (1, 2, 3):
                token_half(dest(0), k, 1).start()

    def edge_cot(q):
        return remote(
            cotg.at[q, my_rows()], cot_edge.at[q, my_rows()], sce, rce, device(z=inward)
        )

    def edge_relay(q, k):
        return remote(
            cot_edge.at[q, my_rows()], cot_edge.at[q, my_rows()], sye, rye.at[q],
            device(y=y_peer(k)),
        )

    def edge_tokens(s, h):
        lanes = pl.ds(h * 128, 128)
        return remote(
            tokg.at[dest(s), :, lanes], tok_edge.at[s - 1, :, lanes],
            ste.at[lax.rem(s, 2)], rte.at[s - 1, h], device(z=inward),
        )

    @pl.when(edge)
    def _():
        for q in range(SUBS):
            edge_cot(q).start()

    def pass_up():
        @pl.when(line > 0)
        def _():
            pl.semaphore_wait(wave_up, 1)

        @pl.when(line < last)
        def _():
            pl.semaphore_signal(wave_up, inc=1, device_id=on_line(line + 1), device_id_type=MESH)

    def pass_down():
        @pl.when(line < last)
        def _():
            pl.semaphore_wait(wave_down, 1)

        @pl.when(line > 0)
        def _():
            pl.semaphore_signal(wave_down, inc=1, device_id=on_line(line - 1), device_id_type=MESH)

    def keep(d, _):
        tokg[d, my_rows(), :] = tok[:, columns_of(y, d)]
        return 0

    lax.fori_loop(0, NZ, keep, 0)

    loads[2].wait()
    loads[3].wait()
    low = lax.broadcasted_iota(jnp.int32, (256, 128), 1) < BLOCK

    def decode(t, _):
        at = pl.ds(pl.multiple_of(t * 128, 128), 128)
        delta = shared[:, at].astype(F32) - w[:, at].astype(F32)
        size = jnp.abs(delta)
        first = jnp.max(jnp.where(low, size, 0.0), axis=1, keepdims=True)
        second = jnp.max(jnp.where(low, 0.0, size), axis=1, keepdims=True)
        largest = jnp.where(low, first, second)
        scale = ((largest + 1e-06) / code_range).astype(BF16).astype(F32)
        coded = (delta / scale).astype(BF16).astype(F32)
        dec[t // 2, :, pl.ds(pl.multiple_of(lax.rem(t, 2) * 128, 128), 128)] = (coded * scale).astype(BF16)
        return 0

    lax.fori_loop(0, 8, decode, 0)

    def scatter_copy(k):
        peer = x_peer(k)
        return remote(dec.at[peer], x_in.at[k - 1], sx, rx, device(x=peer))

    for k in (1, 2, 3):
        scatter_copy(k).start()

    near_half = zh == 0
    pl.when(near_half)(pass_up)

    for q in range(1, SUBS):
        for k in (1, 2, 3):
            cot_copy(q, k).start()

    mine = pl.ds(pl.multiple_of(c * 128, 128), 128)
    other = pl.ds(pl.multiple_of((1 - c) * 128, 128), 128)
    my_lanes = pl.ds(pl.multiple_of(zh * 128, 128), 128)
    far_lanes = pl.ds(pl.multiple_of((1 - zh) * 128, 128), 128)
    core = device(c=1 - c)
    far = device(zh=1 - zh)
    core_sum = remote(core_out, core_in, ss, rs.at[0], core)
    z_sum = remote(z_out, z_in, ss, rs.at[1], far)
    core_full = remote(full.at[mine], full.at[mine], ss, rs.at[2], core)
    core_pair = remote(pair_out, pair_in, ss, rs.at[3], core)
    z_gather = remote(sh.at[x, mine, my_lanes], sh.at[x, mine, my_lanes], ss, rs.at[4], far)
    core_gather = remote(sh.at[:, mine], sh_in, ss, rs.at[5], core)

    def gather_copy(k):
        return remote(sh.at[x, mine], sh.at[x, mine], sg, rg, device(x=x_peer(k)))

    stores = [
        pltpu.make_async_copy(src, dst, out_sem.at[i])
        for i, (src, dst) in enumerate([(master_new, master_out), (mom_new, mom_out)])
    ]

    def stage_x():
        arrived(x_in, rx)

        def summed(rows):
            acc = dec[x, rows, :].astype(F32)
            for k in range(3):
                acc = acc + x_in[k, rows, :].astype(F32)
            return acc

        core_out[...] = summed(other).astype(BF16)
        core_sum.start()
        half[...] = summed(mine)

    def stage_core():
        core_sum.wait_recv()
        half[...] = half[...] + core_in[...].astype(F32)
        z_out[...] = half[:, far_lanes].astype(BF16)
        z_sum.start()

    def stage_far():
        z_sum.wait_recv()
        full[mine, :] = half[:, my_lanes] + z_in[...].astype(F32)
        core_full.start()

    def stage_update():
        core_full.wait_recv()
        loads[4].wait()
        loads[5].wait()
        average = jnp.transpose(full[...]) / float(REPLICAS)
        average = jnp.where(c == 0, average[:BLOCK], average[BLOCK:])
        momentum_next = outer_beta * mom[...] + average
        master_next = master[...] - outer_rate * (average + outer_beta * momentum_next)
        mom_new[...] = momentum_next
        master_new[...] = master_next
        stores[0].start()
        stores[1].start()
        twice = jnp.concatenate([master_next, master_next], axis=0)
        share = lax.broadcasted_iota(jnp.int32, (128, 256), 0) // BLOCK
        pair_out[...] = jnp.transpose(jnp.where(share == c, twice, 0.0)).astype(BF16)
        core_pair.start()

    def stage_pair():
        core_pair.wait_recv()
        sh[x, :, my_lanes] = pair_out[...] + pair_in[...]
        z_gather.start()

    def stage_gather():
        z_gather.wait_recv()
        for k in (1, 2, 3):
            gather_copy(k).start()

    def stage_last():
        arrived(sh_in.at[pl.ds(0, 3)], rg)
        core_gather.start()

    def pick(*choices):
        at = choices[-1]
        for i in range(len(choices) - 1):
            at = jnp.where(depth == i, choices[i], at)
        return at

    def by_place(low, high):
        return jnp.where(low_half, pick(*low), pick(*high))

    up_at = by_place((1, 1, 1, 1), (10, 8, 4, 1))
    down_far = by_place((10, 8, 4, 1), (1, 1, 1, 1))
    down_near = by_place((22, 20, 16, 10), (12, 12, 10, 8))
    core_at = jnp.where(near_half, down_near, jnp.maximum(up_at, 4))
    far_at = jnp.where(
        near_half, by_place((24, 23, 20, 18), (18, 18, 16, 16)), by_place((24, 23, 20, 17), (20, 20, 18, 17))
    )
    gather_at = jnp.where(near_half, by_place((42, 42, 38, 35), (36, 35, 34, 34)), pick(32, 32, 30, 29))
    stages = [
        (2, stage_x),
        (up_at, lambda: pl.when(jnp.logical_not(near_half))(pass_up)),
        (jnp.where(near_half, down_near, down_far), pass_down),
        (core_at, stage_core),
        (far_at, stage_far),
        (far_at + 2, stage_update),
        (far_at + 4, stage_pair),
        (gather_at, stage_gather),
        (gather_at + 4, stage_last),
    ]

    def multiply(rows, columns):
        return lax.dot_general(rows, columns, (((0,), (0,)), ((), ())), preferred_element_type=F32)

    def split(j, by_column):
        h = jnp.where(by_column, lax.rem(j, 2), lax.rem(j // 2, 2))
        q = jnp.where(by_column, j // 2, 2 * (j // SUBS) + lax.rem(j, 2))
        return pl.ds(pl.multiple_of(h * 128, 128), 128), q

    def stream(way, v):
        s, j = v // PARTS, lax.rem(v, PARTS)
        to = jnp.where(way == 0, z + 1, z - 1)
        slot = jnp.where(way == 0, v, NZ * PARTS + PARTS - 1 - v)
        return remote(
            buf.at[way, s, j], buf.at[way, s, j], su.at[way, lax.rem(v, DEPTH)], ru.at[slot], device(z=to)
        )

    count_in = jnp.where(edge, PARTS, PARTS * (NZ - 1 - depth))
    count_out = PARTS * depth
    inner = jnp.where(low_half, 0, 1)

    def wait_first(k, d, h):
        @pl.when(k == 0)
        def _():
            wait_half(h)

        if h == 0:
            pl.when(k == 1)(lambda: wait_tokens(d))

    def unit(k, u):
        way = jnp.where(k == 0, inner, 1 - inner)
        v = jnp.where(k == 0, u, u - (36 - 10 * depth))

        @pl.when((v >= 0) & (v < jnp.where(k == 0, count_in, count_out)))
        def _():
            s, j = v // PARTS, lax.rem(v, PARTS)
            d = jnp.where(way == 0, NZ - 1 - s, s)
            rows, q = split(j, s == 0)
            joined = (k == 0) & second & (s > 0)

            @pl.when(s == 0)
            def _():
                for h in range(2):
                    pl.when(j == h)(lambda: wait_first(k, d, h))

            @pl.when((s > 0) & (j == 0))
            def _():
                wait_tokens(d)

            acc[...] = multiply(tokg[d, :, rows], cotg[q])

            @pl.when(joined)
            def _():
                for h in range(2):
                    pl.when(j == 2 * h)(lambda: edge_tokens(s, h).wait_recv())

                @pl.when((s == 1) & (lax.rem(j // 2, 2) == 0))
                def _():
                    arrived(cot_edge.at[q, three], rye.at[q])

                acc[...] += multiply(tok_edge[s - 1, :, rows], cot_edge[q])

            @pl.when(jnp.logical_not(joined | (edge & (k == 0))))
            def _():
                stream(way, v).wait_recv()
                acc[...] += buf[way, s, j].astype(F32)

            buf[way, s, j] = acc[...].astype(BF16)

            @pl.when(v >= DEPTH)
            def _():
                stream(way, v - DEPTH).wait_send()

            stream(way, v).start()

    def forward_tokens(u):
        s = (u - PARTS) // 4 + 1

        @pl.when(edge & (u >= PARTS) & (s < NZ - 1) & (lax.rem(u, 4) == 0))
        def _():
            wait_tokens(dest(s))

            @pl.when(s >= 3)
            def _():
                departed(tokg.at[0], ste.at[lax.rem(s, 2)])

            for h in range(2):
                edge_tokens(s, h).start()

    relays = jnp.where(second, SUBS, 0)

    def y_job(u):
        i = u // 2

        @pl.when((lax.rem(u, 2) == 0) & (i <= NZ - 2 + relays))
        def _():
            pl.when(i == 0)(lambda: send_tokens(dest(1)))

            @pl.when((i > 0) & (i <= relays))
            def _():
                pl.when(i == 1)(lambda: arrived(cot_edge.at[:, my_rows()], rce))
                for k in (1, 2, 3):
                    edge_relay(i - 1, k).start()

            pl.when(i > relays)(lambda: send_tokens(dest(order(i - relays + 1))))

    def step(u, _):
        @pl.when((u < PARTS) & (lax.rem(u, 2) == 0))
        def _():
            wait_cots(u // 2)

        def both(k, _):
            unit(k, u)
            return 0

        lax.fori_loop(0, 2, both, 0)
        forward_tokens(u)

        y_job(u)
        for at, stage in stages:
            pl.when(u == at)(stage)
        return 0

    lax.fori_loop(0, UNITS, step, 0)

    wait_tokens(z)

    @pl.when(second)
    def _():
        for h in range(2):
            edge_tokens(NZ - 2, h).wait_recv()

    core_gather.wait_recv()
    for q in range(SUBS):
        sh[q, other, :] = sh_in[q]
    row = lax.broadcasted_iota(jnp.int32, (64, 128), 0)
    gain = gain_ref[...].astype(F32) * (mix_weight * inner_gain / math.sqrt(32 * 128))
    for h in range(2):
        line_gain = jnp.sum(jnp.where(row == 2 * fs + h, gain, 0.0), axis=0, keepdims=True)
        tall = jnp.transpose(jnp.broadcast_to(line_gain, (128, 128)))
        rates[pl.ds(h * 128, 128), :] = jnp.concatenate([tall, tall], axis=1)

    def prepare(j, _):
        rows, q = split(j, edge)
        at = pl.ds(pl.multiple_of(q * COLS, COLS), COLS)
        acc[...] = multiply(tokg[z, :, rows], cotg[q])

        @pl.when(second)
        def _():
            acc[...] += multiply(tok_edge[NZ - 3, :, rows], cot_edge[q])

        half_w = mix_weight * w[rows, at].astype(F32) + (1.0 - mix_weight) * sh[q, rows, :].astype(F32)
        own[j] = half_w - rates[rows, :] * acc[...]
        return 0

    lax.fori_loop(0, PARTS, prepare, 0)

    def finish(j, _):
        rows, q = split(j, edge)
        at = pl.ds(pl.multiple_of(q * COLS, COLS), COLS)

        @pl.when(z > 1)
        def _():
            stream(0, (NZ - 1 - z) * PARTS + j).wait_recv()
            own[j] -= rates[rows, :] * buf[0, NZ - 1 - z, j].astype(F32)

        @pl.when(z < NZ - 2)
        def _():
            stream(1, z * PARTS + j).wait_recv()
            own[j] -= rates[rows, :] * buf[1, z, j].astype(F32)

        layer[rows, at] = own[j].astype(BF16)
        pltpu.make_async_copy(layer.at[rows, at], layer_out.at[rows, at], out_sem.at[2]).start()
        return 0

    lax.fori_loop(0, PARTS, finish, 0)
    departed(tok.at[:, pl.ds(0, 6144)], st)
    departed(cotg.at[pl.ds(0, 3)], sc)
    departed(dec.at[pl.ds(0, 3)], sx)
    departed(sh_in.at[pl.ds(0, 3)], sg)
    departed(dec, ss)
    for store in stores:
        store.wait()
    pltpu.make_async_copy(layer, layer_out, out_sem.at[2]).wait()

    for back in range(1, DEPTH + 1):
        stream(inner, count_in - back).wait_send()

    @pl.when(depth > 0)
    def _():
        for back in range(1, DEPTH + 1):
            stream(1 - inner, count_out - back).wait_send()

    @pl.when(edge)
    def _():
        departed(cotg.at[0], sce)
        for s in range(2):
            departed(tokg.at[0], ste.at[s])

    @pl.when(second)
    def _():
        departed(cot_edge.at[pl.ds(0, 3)], sye)


def copy_kernel(*refs):
    ins, outs, held, sem_in, sem_out = refs[:3], refs[3:6], refs[6:9], refs[9], refs[10]
    pieces = [(0, pl.ds(i * 64, 64)) for i in range(4)] + [(1, pl.ds(0, 64)), (2, pl.ds(0, 64))]
    fetch = [
        pltpu.make_async_copy(ins[n].at[at], held[n].at[at], sem_in.at[i]) for i, (n, at) in enumerate(pieces)
    ]
    write = [
        pltpu.make_async_copy(held[n].at[at], outs[n].at[at], sem_out.at[i]) for i, (n, at) in enumerate(pieces)
    ]
    for copy in fetch:
        copy.start()
    for a, b in zip(fetch, write):
        a.wait()
        b.start()
    for copy in write:
        copy.wait()


def on_device(tokens, norm_gain, cotangent, layer_weight, shared_copy, master, momentum):
    vmem, hbm = pltpu.VMEM, pl.ANY
    dma = pltpu.SemaphoreType.DMA
    scratch = [
        vmem((128, 8192), BF16), vmem((128, 1024), BF16), vmem((256, 1024), BF16), vmem((256, 1024), BF16),
        vmem((64, 256), F32), vmem((64, 256), F32),
        vmem((256, 1024), BF16), vmem((64, 256), F32), vmem((64, 256), F32),
        vmem((NZ, 512, COLS), BF16), vmem((SUBS, 512, COLS), BF16),
        vmem((2, NZ - 1, PARTS, 128, COLS), BF16), vmem((128, COLS), F32),
        vmem((PARTS, 128, COLS), F32), vmem((256, COLS), F32),
        vmem((NZ - 2, 512, COLS), BF16), vmem((SUBS, 512, COLS), BF16),
        vmem((4, 256, 256), BF16), vmem((3, 256, 256), BF16), vmem((128, 256), F32),
        vmem((128, 256), BF16), vmem((128, 256), BF16), vmem((128, 128), BF16), vmem((128, 128), BF16),
        vmem((256, 128), F32), vmem((256, 128), BF16), vmem((256, 128), BF16),
        vmem((4, 256, 256), BF16), vmem((4, 128, 256), BF16),
        dma((6,)), dma, dma((NZ + 1,)), dma, dma((SUBS,)),
        dma((2, DEPTH)), dma(((NZ + 1) * PARTS,)),
        dma((2,)), dma((NZ - 2, 2)), dma, dma, dma, dma((SUBS,)),
        dma, dma, dma, dma, dma, dma((6,)), dma((3,)),
        pltpu.SemaphoreType.REGULAR, pltpu.SemaphoreType.REGULAR,
    ]
    layer_next, master_next, momentum_next = pl.pallas_call(
        kernel,
        out_shape=[
            jax.ShapeDtypeStruct((256, 1024), BF16),
            jax.ShapeDtypeStruct((64, 256), F32),
            jax.ShapeDtypeStruct((64, 256), F32),
        ],
        in_specs=[pl.BlockSpec(memory_space=hbm), pl.BlockSpec(memory_space=vmem)]
        + [pl.BlockSpec(memory_space=hbm)] * 5,
        out_specs=[pl.BlockSpec(memory_space=hbm)] * 3,
        scratch_shapes=scratch,
        name="diloco_step",
        cost_estimate=pl.CostEstimate(flops=2 * 4096 * 256 * 1024, bytes_accessed=5 << 20, transcendentals=0),
        compiler_params=pltpu.CompilerParams(
            collective_id=0, has_side_effects=True, vmem_limit_bytes=60 << 20
        ),
    )(
        tokens[0], norm_gain.reshape(64, 128), cotangent[0], layer_weight[0], shared_copy, master.T, momentum.T
    )
    results = (layer_next, master_next, momentum_next)
    layer_next, master_next, momentum_next = pl.pallas_call(
        copy_kernel,
        out_shape=[jax.ShapeDtypeStruct(r.shape, r.dtype) for r in results],
        in_specs=[pl.BlockSpec(memory_space=hbm)] * 3,
        out_specs=[pl.BlockSpec(memory_space=hbm)] * 3,
        scratch_shapes=[vmem(r.shape, r.dtype) for r in results] + [dma((6,)), dma((6,))],
        name="write_out",
        compiler_params=pltpu.CompilerParams(vmem_limit_bytes=60 << 20),
    )(*results)
    return (layer_next[None], master_next.T, momentum_next.T)


def solution(mesh):
    in_specs = (
        P("replica", "fsdp", None),
        P(),
        P("replica", "fsdp", None),
        P("replica", "fsdp", None),
        P("fsdp", None),
        P("fsdp", "replica"),
        P("fsdp", "replica"),
    )
    out_specs = (P("replica", "fsdp", None), P("fsdp", "replica"), P("fsdp", "replica"))
    return jax.shard_map(
        on_device, mesh=mesh, in_specs=in_specs, out_specs=out_specs, check_vma=False
    )
```

```python
import functools
import math

import jax
import jax.numpy as jnp
from jax import lax
from jax.experimental import pallas as pl
from jax.experimental.pallas import tpu as pltpu
from jax.sharding import PartitionSpec as P

BLOCK = 64
norm_eps = 1e-05
inner_gain = 0.4
outer_rate = 0.7
outer_beta = 0.9
mix_weight = 0.5
code_range = 448.0

NX, NY, NZ = 4, 4, 8
REPLICAS = 16
MESH = pl.DeviceIdType.MESH
F32, BF16 = jnp.float32, jnp.bfloat16
COLS = 256
SUBS = 4
PARTS = 2 * SUBS
UNITS = (NZ - 1) * PARTS
DEPTH = 8


def kernel(
    tok_hbm, gain_ref, cot_hbm, w_hbm, shared_hbm, master_hbm, mom_hbm,
    layer_out, master_out, mom_out,
    tok, cot, w, shared, master, mom, layer, master_new, mom_new,
    tokg, cotg, buf, acc, own, rates, tok_edge, cot_edge, dec, x_in, half, core_out, core_in, z_out, z_in,
    full, pair_out, pair_in, sh, sh_in,
    load_sem, st, rt, sc, rc, su, ru, ste, rte, sce, rce, sye, rye, sx, rx, sg, rg, ss, rs, out_sem, wave_up, wave_down,
):
    rep, fs = lax.axis_index("replica"), lax.axis_index("fsdp")
    x, zh, c = rep // 4, lax.rem(rep // 2, 2), lax.rem(rep, 2)
    y, z = fs // NZ, lax.rem(fs, NZ)
    line = zh * NZ + z
    last = 2 * NZ - 1
    low_half = z < NZ // 2
    depth = jnp.where(low_half, z, NZ - 1 - z)
    inward = jnp.where(low_half, z + 1, z - 1)
    edge, second = depth == 0, depth == 1

    def device(x=x, zh=zh, c=c, y=y, z=z):
        return (x * 4 + zh * 2 + c, y * NZ + z)

    def on_line(at):
        return device(zh=at // NZ, z=lax.rem(at, NZ))

    def y_peer(k):
        return lax.rem(y + k, NY)

    def x_peer(k):
        return lax.rem(x + k, NX)

    loads = [
        pltpu.make_async_copy(src, dst, load_sem.at[i])
        for i, (src, dst) in enumerate(
            [(tok_hbm, tok), (cot_hbm, cot), (w_hbm, w), (shared_hbm, shared),
             (master_hbm, master), (mom_hbm, mom)]
        )
    ]
    loads[0].start()
    loads[1].start()
    barrier = pltpu.get_barrier_semaphore()

    def greet(where):
        pl.semaphore_signal(barrier, inc=1, device_id=where, device_id_type=MESH)

    for k in (1, 2, 3):
        greet(device(y=y_peer(k)))
        greet(device(x=x_peer(k)))
    greet(device(c=1 - c))

    @pl.when(line > 0)
    def _():
        greet(on_line(line - 1))

    @pl.when(line < last)
    def _():
        greet(on_line(line + 1))

    def remote(src, dst, send, recv, where):
        return pltpu.make_async_remote_copy(
            src_ref=src, dst_ref=dst, send_sem=send, recv_sem=recv, device_id=where, device_id_type=MESH
        )

    def dest(s):
        return jnp.where(low_half, NZ - 1 - s, s)

    def order(i):
        return jnp.where(lax.rem(i, 2) == 0, 1 + i // 2, NZ - 1 - (i - 3) // 2)

    def my_rows():
        return pl.ds(pl.multiple_of(y * 128, 128), 128)

    def columns_of(peer, d):
        return pl.ds(pl.multiple_of((peer * NZ + d) * COLS, COLS), COLS)

    def half_columns(peer, d, h):
        return pl.ds(pl.multiple_of((peer * NZ + d) * COLS + h * 128, 128), 128)

    def token_copy(d, k):
        peer = y_peer(k)
        return remote(tok.at[:, columns_of(peer, d)], tokg.at[d, my_rows()], st, rt.at[d], device(y=peer))

    def token_half(d, k, h):
        peer = y_peer(k)
        return remote(
            tok.at[:, half_columns(peer, d, h)], tokg.at[d, my_rows(), pl.ds(h * 128, 128)],
            st, rt.at[d if h == 0 else NZ], device(y=peer),
        )

    def cot_copy(q, k):
        return remote(cotg.at[q, my_rows()], cotg.at[q, my_rows()], sc, rc.at[q], device(y=y_peer(k)))

    def arrived(ref, sem):
        remote(ref, ref, st, sem, device(y=y_peer(1))).wait_recv()

    def departed(ref, sem):
        remote(ref, ref, sem, rt.at[0], device(y=y_peer(1))).wait_send()

    three = pl.ds(0, 3 * 128)

    def wait_half(h):
        d = dest(0)
        arrived(tokg.at[d, three, pl.ds(h * 128, 128)], rt.at[d if h == 0 else NZ])

    def send_tokens(d):
        for k in (1, 2, 3):
            token_copy(d, k).start()

    def wait_tokens(d):
        arrived(tokg.at[d, three], rt.at[d])

    def wait_cots(q):
        arrived(cotg.at[q, three], rc.at[q])

    loads[0].wait()
    pl.semaphore_wait(barrier, 7 + jnp.where(line > 0, 1, 0) + jnp.where(line < last, 1, 0))
    for k in (1, 2, 3):
        token_half(dest(0), k, 0).start()
    for load in loads[2:]:
        load.start()

    def square(j, acc):
        t = tok[:, pl.ds(pl.multiple_of(j * 128, 128), 128)].astype(F32)
        return acc + t * t

    total = lax.fori_loop(0, 64, square, jnp.zeros((128, 128), F32), unroll=8)
    inverse = lax.rsqrt(jnp.sum(total, axis=1, keepdims=True) / 8192.0 + norm_eps)
    loads[1].wait()
    for q in range(SUBS):
        cotg[q, my_rows(), :] = (cot[:, q * COLS : (q + 1) * COLS].astype(F32) * inverse).astype(BF16)
        if q == 0:
            for k in (1, 2, 3):
                cot_copy(q, k).start()
            for k in (1, 2, 3):
                token_half(dest(0), k, 1).start()

    def edge_cot(q):
        return remote(
            cotg.at[q, my_rows()], cot_edge.at[q, my_rows()], sce, rce, device(z=inward)
        )

    def edge_relay(q, k):
        return remote(
            cot_edge.at[q, my_rows()], cot_edge.at[q, my_rows()], sye, rye.at[q],
            device(y=y_peer(k)),
        )

    def edge_tokens(s, h):
        lanes = pl.ds(h * 128, 128)
        return remote(
            tokg.at[dest(s), :, lanes], tok_edge.at[s - 1, :, lanes],
            ste.at[lax.rem(s, 2)], rte.at[s - 1, h], device(z=inward),
        )

    @pl.when(edge)
    def _():
        for q in range(SUBS):
            edge_cot(q).start()

    def pass_up():
        @pl.when(line > 0)
        def _():
            pl.semaphore_wait(wave_up, 1)

        @pl.when(line < last)
        def _():
            pl.semaphore_signal(wave_up, inc=1, device_id=on_line(line + 1), device_id_type=MESH)

    def pass_down():
        @pl.when(line < last)
        def _():
            pl.semaphore_wait(wave_down, 1)

        @pl.when(line > 0)
        def _():
            pl.semaphore_signal(wave_down, inc=1, device_id=on_line(line - 1), device_id_type=MESH)

    def keep(d, _):
        tokg[d, my_rows(), :] = tok[:, columns_of(y, d)]
        return 0

    lax.fori_loop(0, NZ, keep, 0)

    loads[2].wait()
    loads[3].wait()
    low = lax.broadcasted_iota(jnp.int32, (256, 128), 1) < BLOCK

    def decode(t, _):
        at = pl.ds(pl.multiple_of(t * 128, 128), 128)
        delta = shared[:, at].astype(F32) - w[:, at].astype(F32)
        size = jnp.abs(delta)
        first = jnp.max(jnp.where(low, size, 0.0), axis=1, keepdims=True)
        second = jnp.max(jnp.where(low, 0.0, size), axis=1, keepdims=True)
        largest = jnp.where(low, first, second)
        scale = ((largest + 1e-06) / code_range).astype(BF16).astype(F32)
        coded = (delta / scale).astype(BF16).astype(F32)
        dec[t // 2, :, pl.ds(pl.multiple_of(lax.rem(t, 2) * 128, 128), 128)] = (coded * scale).astype(BF16)
        return 0

    lax.fori_loop(0, 8, decode, 0)

    def scatter_copy(k):
        peer = x_peer(k)
        return remote(dec.at[peer], x_in.at[k - 1], sx, rx, device(x=peer))

    for k in (1, 2, 3):
        scatter_copy(k).start()

    near_half = zh == 0
    pl.when(near_half)(pass_up)

    for q in range(1, SUBS):
        for k in (1, 2, 3):
            cot_copy(q, k).start()

    mine = pl.ds(pl.multiple_of(c * 128, 128), 128)
    other = pl.ds(pl.multiple_of((1 - c) * 128, 128), 128)
    my_lanes = pl.ds(pl.multiple_of(zh * 128, 128), 128)
    far_lanes = pl.ds(pl.multiple_of((1 - zh) * 128, 128), 128)
    core = device(c=1 - c)
    far = device(zh=1 - zh)
    core_sum = remote(core_out, core_in, ss, rs.at[0], core)
    z_sum = remote(z_out, z_in, ss, rs.at[1], far)
    core_full = remote(full.at[mine], full.at[mine], ss, rs.at[2], core)
    core_pair = remote(pair_out, pair_in, ss, rs.at[3], core)
    z_gather = remote(sh.at[x, mine, my_lanes], sh.at[x, mine, my_lanes], ss, rs.at[4], far)
    core_gather = remote(sh.at[:, mine], sh_in, ss, rs.at[5], core)

    def gather_copy(k):
        return remote(sh.at[x, mine], sh.at[x, mine], sg, rg, device(x=x_peer(k)))

    stores = [
        pltpu.make_async_copy(src, dst, out_sem.at[i])
        for i, (src, dst) in enumerate([(master_new, master_out), (mom_new, mom_out)])
    ]

    def stage_x():
        arrived(x_in, rx)

        def summed(rows):
            acc = dec[x, rows, :].astype(F32)
            for k in range(3):
                acc = acc + x_in[k, rows, :].astype(F32)
            return acc

        core_out[...] = summed(other).astype(BF16)
        core_sum.start()
        half[...] = summed(mine)

    def stage_core():
        core_sum.wait_recv()
        half[...] = half[...] + core_in[...].astype(F32)
        z_out[...] = half[:, far_lanes].astype(BF16)
        z_sum.start()

    def stage_far():
        z_sum.wait_recv()
        full[mine, :] = half[:, my_lanes] + z_in[...].astype(F32)
        core_full.start()

    def stage_update():
        core_full.wait_recv()
        loads[4].wait()
        loads[5].wait()
        average = jnp.transpose(full[...]) / float(REPLICAS)
        average = jnp.where(c == 0, average[:BLOCK], average[BLOCK:])
        momentum_next = outer_beta * mom[...] + average
        master_next = master[...] - outer_rate * (average + outer_beta * momentum_next)
        mom_new[...] = momentum_next
        master_new[...] = master_next
        stores[0].start()
        stores[1].start()
        twice = jnp.concatenate([master_next, master_next], axis=0)
        share = lax.broadcasted_iota(jnp.int32, (128, 256), 0) // BLOCK
        pair_out[...] = jnp.transpose(jnp.where(share == c, twice, 0.0)).astype(BF16)
        core_pair.start()

    def stage_pair():
        core_pair.wait_recv()
        sh[x, :, my_lanes] = pair_out[...] + pair_in[...]
        z_gather.start()

    def stage_gather():
        z_gather.wait_recv()
        for k in (1, 2, 3):
            gather_copy(k).start()

    def stage_last():
        arrived(sh_in.at[pl.ds(0, 3)], rg)
        core_gather.start()

    def pick(*choices):
        at = choices[-1]
        for i in range(len(choices) - 1):
            at = jnp.where(depth == i, choices[i], at)
        return at

    def by_place(low, high):
        return jnp.where(low_half, pick(*low), pick(*high))

    up_at = by_place((1, 1, 1, 1), (10, 8, 4, 1))
    down_far = by_place((10, 8, 4, 1), (1, 1, 1, 1))
    down_near = by_place((22, 20, 16, 10), (12, 12, 10, 8))
    core_at = jnp.where(near_half, down_near, jnp.maximum(up_at, 4))
    far_at = jnp.where(
        near_half, by_place((24, 23, 20, 18), (18, 18, 16, 16)), by_place((24, 23, 20, 17), (20, 20, 18, 17))
    )
    gather_at = jnp.where(near_half, by_place((42, 42, 38, 35), (36, 35, 34, 34)), pick(32, 32, 30, 29))
    stages = [
        (2, stage_x),
        (up_at, lambda: pl.when(jnp.logical_not(near_half))(pass_up)),
        (jnp.where(near_half, down_near, down_far), pass_down),
        (core_at, stage_core),
        (far_at, stage_far),
        (far_at + 2, stage_update),
        (far_at + 4, stage_pair),
        (gather_at, stage_gather),
        (gather_at + 4, stage_last),
    ]

    def multiply(rows, columns):
        return lax.dot_general(rows, columns, (((0,), (0,)), ((), ())), preferred_element_type=F32)

    def split(j, by_column):
        h = jnp.where(by_column, lax.rem(j, 2), lax.rem(j // 2, 2))
        q = jnp.where(by_column, j // 2, 2 * (j // SUBS) + lax.rem(j, 2))
        return pl.ds(pl.multiple_of(h * 128, 128), 128), q

    def stream(way, v):
        s, j = v // PARTS, lax.rem(v, PARTS)
        up = ((way == 0) & (z < NZ - 1)) | (z == 0)
        to = jnp.where(up, z + 1, z - 1)
        slot = jnp.where(way == 0, v, NZ * PARTS + PARTS - 1 - v)
        return remote(
            buf.at[way, s, j], buf.at[way, s, j], su.at[way, lax.rem(v, DEPTH)], ru.at[slot], device(z=to)
        )

    count_in = jnp.where(edge, PARTS, PARTS * (NZ - 1 - depth))
    count_out = PARTS * depth
    inner = jnp.where(low_half, 0, 1)

    def wait_first(k, d, h):
        @pl.when(k == 0)
        def _():
            wait_half(h)

        if h == 0:
            pl.when(k == 1)(lambda: wait_tokens(d))

    def unit(k, u):
        way = jnp.where(k == 0, inner, 1 - inner)
        v = jnp.where(k == 0, u, u - (36 - 10 * depth))

        @pl.when((v >= 0) & (v < jnp.where(k == 0, count_in, count_out)))
        def _():
            s, j = v // PARTS, lax.rem(v, PARTS)
            d = jnp.where(way == 0, NZ - 1 - s, s)
            rows, q = split(j, s == 0)
            joined = (k == 0) & second & (s > 0)

            @pl.when(s == 0)
            def _():
                for h in range(2):
                    pl.when(j == h)(lambda: wait_first(k, d, h))

            @pl.when((s > 0) & (j == 0))
            def _():
                wait_tokens(d)

            acc[...] = multiply(tokg[d, :, rows], cotg[q])

            @pl.when(joined)
            def _():
                for h in range(2):
                    pl.when(j == 2 * h)(lambda: edge_tokens(s, h).wait_recv())

                @pl.when((s == 1) & (lax.rem(j // 2, 2) == 0))
                def _():
                    arrived(cot_edge.at[q, three], rye.at[q])

                acc[...] += multiply(tok_edge[s - 1, :, rows], cot_edge[q])

            @pl.when(jnp.logical_not(joined | (edge & (k == 0))))
            def _():
                stream(way, v).wait_recv()
                acc[...] += buf[way, s, j].astype(F32)

            buf[way, s, j] = acc[...].astype(BF16)

            @pl.when(v >= DEPTH)
            def _():
                stream(way, v - DEPTH).wait_send()

            stream(way, v).start()

    def forward_tokens(u):
        s = (u - PARTS) // 4 + 1

        @pl.when(edge & (u >= PARTS) & (s < NZ - 1) & (lax.rem(u, 4) == 0))
        def _():
            wait_tokens(dest(s))

            @pl.when(s >= 3)
            def _():
                departed(tokg.at[0], ste.at[lax.rem(s, 2)])

            for h in range(2):
                edge_tokens(s, h).start()

    relays = jnp.where(second, SUBS, 0)

    def y_job(u):
        i = u // 2

        @pl.when((lax.rem(u, 2) == 0) & (i <= NZ - 2 + relays))
        def _():
            pl.when(i == 0)(lambda: send_tokens(dest(1)))

            @pl.when((i > 0) & (i <= relays))
            def _():
                pl.when(i == 1)(lambda: arrived(cot_edge.at[:, my_rows()], rce))
                for k in (1, 2, 3):
                    edge_relay(i - 1, k).start()

            pl.when(i > relays)(lambda: send_tokens(dest(order(i - relays + 1))))

    def step(u, _):
        @pl.when((u < PARTS) & (lax.rem(u, 2) == 0))
        def _():
            wait_cots(u // 2)

        def both(k, _):
            unit(k, u)
            return 0

        lax.fori_loop(0, 2, both, 0)
        forward_tokens(u)

        y_job(u)
        for at, stage in stages:
            pl.when(u == at)(stage)
        return 0

    lax.fori_loop(0, UNITS, step, 0)

    wait_tokens(z)

    @pl.when(second)
    def _():
        for h in range(2):
            edge_tokens(NZ - 2, h).wait_recv()

    core_gather.wait_recv()
    for q in range(SUBS):
        sh[q, other, :] = sh_in[q]
    row = lax.broadcasted_iota(jnp.int32, (64, 128), 0)
    gain = gain_ref[...].astype(F32) * (mix_weight * inner_gain / math.sqrt(32 * 128))
    for h in range(2):
        line_gain = jnp.sum(jnp.where(row == 2 * fs + h, gain, 0.0), axis=0, keepdims=True)
        tall = jnp.transpose(jnp.broadcast_to(line_gain, (128, 128)))
        rates[pl.ds(h * 128, 128), :] = jnp.concatenate([tall, tall], axis=1)

    def prepare(j, _):
        rows, q = split(j, edge)
        at = pl.ds(pl.multiple_of(q * COLS, COLS), COLS)
        acc[...] = multiply(tokg[z, :, rows], cotg[q])

        @pl.when(second)
        def _():
            acc[...] += multiply(tok_edge[NZ - 3, :, rows], cot_edge[q])

        half_w = mix_weight * w[rows, at].astype(F32) + (1.0 - mix_weight) * sh[q, rows, :].astype(F32)
        own[j] = half_w - rates[rows, :] * acc[...]
        return 0

    lax.fori_loop(0, PARTS, prepare, 0)

    def finish(j, _):
        rows, q = split(j, edge)
        at = pl.ds(pl.multiple_of(q * COLS, COLS), COLS)

        @pl.when(z > 1)
        def _():
            stream(0, (NZ - 1 - z) * PARTS + j).wait_recv()
            own[j] -= rates[rows, :] * buf[0, NZ - 1 - z, j].astype(F32)

        @pl.when(z < NZ - 2)
        def _():
            stream(1, z * PARTS + j).wait_recv()
            own[j] -= rates[rows, :] * buf[1, z, j].astype(F32)

        layer[rows, at] = own[j].astype(BF16)
        pltpu.make_async_copy(layer.at[rows, at], layer_out.at[rows, at], out_sem.at[2]).start()
        return 0

    lax.fori_loop(0, PARTS, finish, 0)
    departed(tok.at[:, pl.ds(0, 6144)], st)
    departed(cotg.at[pl.ds(0, 3)], sc)
    departed(dec.at[pl.ds(0, 3)], sx)
    departed(sh_in.at[pl.ds(0, 3)], sg)
    departed(dec, ss)
    for store in stores:
        store.wait()
    pltpu.make_async_copy(layer, layer_out, out_sem.at[2]).wait()

    for back in range(1, DEPTH + 1):
        stream(inner, count_in - back).wait_send()

    @pl.when(depth > 0)
    def _():
        for back in range(1, DEPTH + 1):
            stream(1 - inner, count_out - back).wait_send()

    @pl.when(edge)
    def _():
        departed(cotg.at[0], sce)
        for s in range(2):
            departed(tokg.at[0], ste.at[s])

    @pl.when(second)
    def _():
        departed(cot_edge.at[pl.ds(0, 3)], sye)


def copy_kernel(*refs):
    ins, outs, held, sem_in, sem_out = refs[:3], refs[3:6], refs[6:9], refs[9], refs[10]
    pieces = [(0, pl.ds(i * 64, 64)) for i in range(4)] + [(1, pl.ds(0, 64)), (2, pl.ds(0, 64))]
    fetch = [
        pltpu.make_async_copy(ins[n].at[at], held[n].at[at], sem_in.at[i]) for i, (n, at) in enumerate(pieces)
    ]
    write = [
        pltpu.make_async_copy(held[n].at[at], outs[n].at[at], sem_out.at[i]) for i, (n, at) in enumerate(pieces)
    ]
    for copy in fetch:
        copy.start()
    for a, b in zip(fetch, write):
        a.wait()
        b.start()
    for copy in write:
        copy.wait()


def on_device(tokens, norm_gain, cotangent, layer_weight, shared_copy, master, momentum):
    vmem, hbm = pltpu.VMEM, pl.ANY
    dma = pltpu.SemaphoreType.DMA
    scratch = [
        vmem((128, 8192), BF16), vmem((128, 1024), BF16), vmem((256, 1024), BF16), vmem((256, 1024), BF16),
        vmem((64, 256), F32), vmem((64, 256), F32),
        vmem((256, 1024), BF16), vmem((64, 256), F32), vmem((64, 256), F32),
        vmem((NZ, 512, COLS), BF16), vmem((SUBS, 512, COLS), BF16),
        vmem((2, NZ - 1, PARTS, 128, COLS), BF16), vmem((128, COLS), F32),
        vmem((PARTS, 128, COLS), F32), vmem((256, COLS), F32),
        vmem((NZ - 2, 512, COLS), BF16), vmem((SUBS, 512, COLS), BF16),
        vmem((4, 256, 256), BF16), vmem((3, 256, 256), BF16), vmem((128, 256), F32),
        vmem((128, 256), BF16), vmem((128, 256), BF16), vmem((128, 128), BF16), vmem((128, 128), BF16),
        vmem((256, 128), F32), vmem((256, 128), BF16), vmem((256, 128), BF16),
        vmem((4, 256, 256), BF16), vmem((4, 128, 256), BF16),
        dma((6,)), dma, dma((NZ + 1,)), dma, dma((SUBS,)),
        dma((2, DEPTH)), dma(((NZ + 1) * PARTS,)),
        dma((2,)), dma((NZ - 2, 2)), dma, dma, dma, dma((SUBS,)),
        dma, dma, dma, dma, dma, dma((6,)), dma((3,)),
        pltpu.SemaphoreType.REGULAR, pltpu.SemaphoreType.REGULAR,
    ]
    layer_next, master_next, momentum_next = pl.pallas_call(
        kernel,
        out_shape=[
            jax.ShapeDtypeStruct((256, 1024), BF16),
            jax.ShapeDtypeStruct((64, 256), F32),
            jax.ShapeDtypeStruct((64, 256), F32),
        ],
        in_specs=[pl.BlockSpec(memory_space=hbm), pl.BlockSpec(memory_space=vmem)]
        + [pl.BlockSpec(memory_space=hbm)] * 5,
        out_specs=[pl.BlockSpec(memory_space=hbm)] * 3,
        scratch_shapes=scratch,
        name="diloco_step",
        cost_estimate=pl.CostEstimate(flops=2 * 4096 * 256 * 1024, bytes_accessed=5 << 20, transcendentals=0),
        compiler_params=pltpu.CompilerParams(
            collective_id=0, has_side_effects=True, vmem_limit_bytes=60 << 20
        ),
    )(
        tokens[0], norm_gain.reshape(64, 128), cotangent[0], layer_weight[0], shared_copy, master.T, momentum.T
    )
    results = (layer_next, master_next, momentum_next)
    layer_next, master_next, momentum_next = pl.pallas_call(
        copy_kernel,
        out_shape=[jax.ShapeDtypeStruct(r.shape, r.dtype) for r in results],
        in_specs=[pl.BlockSpec(memory_space=hbm)] * 3,
        out_specs=[pl.BlockSpec(memory_space=hbm)] * 3,
        scratch_shapes=[vmem(r.shape, r.dtype) for r in results] + [dma((6,)), dma((6,))],
        name="write_out",
        compiler_params=pltpu.CompilerParams(vmem_limit_bytes=60 << 20),
    )(*results)
    return (layer_next[None], master_next.T, momentum_next.T)


def solution(mesh):
    in_specs = (
        P("replica", "fsdp", None),
        P(),
        P("replica", "fsdp", None),
        P("replica", "fsdp", None),
        P("fsdp", None),
        P("fsdp", "replica"),
        P("fsdp", "replica"),
    )
    out_specs = (P("replica", "fsdp", None), P("fsdp", "replica"), P("fsdp", "replica"))
    return jax.shard_map(
        on_device, mesh=mesh, in_specs=in_specs, out_specs=out_specs, check_vma=False
    )
```
